128 devices in a mesh: lon: 32 (over z_hi, x, y), lat: 4 (over z_lo, core).
Axes of the slice: x: 4, y: 4, z: 4 (z_hi: 2, z_lo: 2; z = z_hi * 2 + z_lo), core: 2. Of those that a mesh axis runs over, the one named last changes fastest.
Arguments:
- patch_rows: bfloat16 [262144, 512], P(('lon', 'lat')), may hold values from -400 to 400
- source_embed: bfloat16 [4, 512], replicated, may hold values from -6 to 6
- cell_embed: bfloat16 [512, 128, 512], P('lon', 'lat'), may hold values from -6 to 6
- level_query: bfloat16 [4, 512], replicated, may hold values from -6 to 6
- margin_rows: int32 [128, 3, 3, 128], P(('lon', 'lat')), may hold values from 0 to 2047, as said below
- margin_counts: int32 [128, 3, 3], P(('lon', 'lat')), may hold values from 0 to 128, as said below
- query_weight: bfloat16 [512, 512], replicated, may hold values from -0.25 to 0.25
- key_weight: bfloat16 [512, 512], replicated, may hold values from -0.25 to 0.25
- value_weight: bfloat16 [512, 512], replicated, may hold values from -0.25 to 0.25
- out_weight: bfloat16 [512, 512], replicated, may hold values from -0.25 to 0.25
- conv_weight: bfloat16 [2, 3, 3, 512, 512], replicated, may hold values from -0.09375 to 0.09375
Outputs:
- latent: bfloat16 [512, 128, 4, 512], P('lon', 'lat')
The draws below stay inside these ranges and needn't reach their ends.
Inputs may be any that keep to these rules, and one draw needn't show every extreme that they name: margin_rows[s, a, b, j] is a local row of device s. `margin_counts`: a list whose source device lies outside the latitude range has count 0; every other list, the owner's own among them, has at least one live row; in every draw some tile owner receives 128 rows from every source device beside it.
All inputs are finite; a program needn't handle non-finite values.
Results may differ from the reference program's by a relative error of at most 0.009.
The reference program's roundings to bfloat16 on the way count: a program that leaves them out, or rounds other values in their place, can miss the bound.
Values may be sent and summed in bfloat16 or wider, within the bound.
No kernel may reach another device: no remote copies, remote signals or barrier semaphores. Data moves between devices by JAX's collectives and lax.ppermute only.
A program may use at most 192 MiB of HBM per device.

```python
import math
import jax
import jax.numpy as jnp
from jax import lax

D = 512
HEADS = 16
SOURCES = 4
SRC_ROWS = 512
CAP = 128
LLON = 16
LLAT = 32
LEVELS = 4
LAYERS = 2
PEERS = 128
P_DEV = 2048
ROWS_ALL = 262144
NLON = 512
NLAT = 128
N_LON = 32
N_LAT = 4


def draw_patch_rows(key, part):
    key = jax.random.fold_in(key, 11)
    first = jax.random.fold_in(key, 0)
    return jax.random.truncated_normal(first, -6.0, 6.0, (ROWS_ALL, D), jnp.float32).astype(jnp.bfloat16)


def draw_margin_rows(key, part):
    key = jax.random.fold_in(key, 12)
    return jax.random.randint(key, (PEERS, 3, 3, CAP), 0, P_DEV, jnp.int32)


def draw_margin_counts(key, part):
    key = jax.random.fold_in(key, 13)
    first, second, third = jax.random.split(key, 3)
    full_owner = jax.random.randint(first, (), 0, PEERS, jnp.int32)
    heavy = jax.random.randint(second, (PEERS, 1, 1), CAP // 2, CAP + 1, jnp.int32)
    heavy = jnp.broadcast_to(heavy, (PEERS, 3, 3))
    counts = jax.random.randint(third, (PEERS, 3, 3), heavy // 2, heavy + 1, jnp.int32)
    counts = jnp.maximum(counts, 1)
    owners = jnp.arange(PEERS, dtype=jnp.int32)[:, None, None]
    counts = jnp.where(owners == full_owner, CAP, counts)
    src_lat = owners % N_LAT + jnp.arange(3, dtype=jnp.int32)[None, None, :] - 1
    inside = (src_lat >= 0) & (src_lat < N_LAT)
    return jnp.where(inside, counts, 0).astype(jnp.int32)


def steps_of(key, shape, cuts, smallest, high):
    loudness, own = 1.0, jax.random.fold_in(key, 6)
    for dim, parts in cuts:
        heights = jnp.exp(jax.random.uniform(jax.random.fold_in(own, dim), (parts,), jnp.float32, smallest / len(cuts), high / len(cuts)))
        loudness = loudness * jnp.repeat(heights, shape[dim] // parts).reshape([-1 if axis == dim else 1 for axis in range(len(shape))])
    return loudness


def normal_values(stream_key, shape, scale, limit, shards=(), kind=jnp.bfloat16):
    level = steps_of(stream_key, shape, shards, -0.22, 0.18) if shards else 1.0
    array = jax.random.normal(stream_key, shape, jnp.float32) * scale * level
    return jnp.minimum(jnp.maximum(array, -limit), limit).astype(kind)


def setup_inputs(seed: int = 0) -> dict:
    streams_of = jax.random.split(jax.random.key(seed), 12)
    return {
        "patch_rows": draw_patch_rows(jax.random.fold_in(streams_of[11], 71), 0),
        "source_embed": normal_values(streams_of[1], (SOURCES, D), 1.0, 6.0),
        "cell_embed": normal_values(streams_of[2], (NLON, NLAT, D), 1.0, 6.0, ((0, 32), (1, 4))),
        "level_query": normal_values(streams_of[3], (LEVELS, D), 1.0, 6.0),
        "margin_rows": draw_margin_rows(jax.random.fold_in(streams_of[11], 71), 0),
        "margin_counts": draw_margin_counts(jax.random.fold_in(streams_of[11], 71), 0),
        "query_weight": normal_values(streams_of[6], (D, D), D ** -0.5, 0.25),
        "key_weight": normal_values(streams_of[7], (D, D), D ** -0.5, 0.25),
        "value_weight": normal_values(streams_of[8], (D, D), D ** -0.5, 0.25),
        "out_weight": normal_values(streams_of[9], (D, D), D ** -0.5, 0.25),
        "conv_weight": normal_values(streams_of[10], (LAYERS, 3, 3, D, D), (9 * D) ** -0.5, 0.09375),
    }


def attend(latent_in, keys, values, valid, query_weight, out_weight):
    count = latent_in.shape[0]
    width = latent_in.shape[1]
    head_size = width // HEADS
    scale = 1.0 / math.sqrt(head_size)
    queries = jnp.dot(latent_in, query_weight, preferred_element_type=jnp.float32).astype(jnp.bfloat16)
    q_heads = queries.reshape(count, HEADS, head_size).transpose(1, 0, 2)
    k_heads = keys.reshape(-1, HEADS, head_size).transpose(1, 0, 2)
    v_heads = values.reshape(-1, HEADS, head_size).transpose(1, 0, 2)

    def one_head(operands):
        q_part, k_part, v_part = operands
        scores = lax.dot_general(q_part.astype(jnp.float32), k_part.astype(jnp.float32), (((1,), (1,)), ((), ())), preferred_element_type=jnp.float32) * scale
        scores = jnp.where(valid[None, :], scores, jnp.float32(-1e+30))
        top = lax.optimization_barrier(jnp.max(scores, axis=1, keepdims=True))
        weights = jnp.exp(scores - top)
        probs = (weights / lax.optimization_barrier(jnp.sum(weights, axis=1, keepdims=True))).astype(jnp.bfloat16)
        return jnp.dot(probs, v_part, preferred_element_type=jnp.float32).astype(jnp.bfloat16)
    heads_out = lax.map(one_head, (q_heads, k_heads, v_heads))
    attended = heads_out.transpose(1, 0, 2).reshape(count, width)
    mixed = latent_in.astype(jnp.float32) + jnp.dot(attended, out_weight, preferred_element_type=jnp.float32)
    return mixed.astype(jnp.bfloat16)

def conv_taps(padded, kernels, cells_lon, cells_lat):
    width = padded.shape[-1]
    total = jnp.zeros((cells_lon * cells_lat * padded.shape[2], width), jnp.float32)
    for row_off in range(3):
        for col_off in range(3):
            window = padded[row_off:row_off + cells_lon, col_off:col_off + cells_lat].reshape(-1, width)
            total = total + jnp.dot(window, kernels[row_off, col_off], preferred_element_type=jnp.float32)
    return total.reshape(cells_lon, cells_lat, padded.shape[2], width)

def normalize(state, cos_gain):
    values = state.astype(jnp.float32)
    spread = jnp.sqrt(lax.optimization_barrier(jnp.mean(values * values, axis=-1, keepdims=True)) + 1e-06)
    return (values / spread * cos_gain[None, :, None, None]).astype(jnp.bfloat16)

def reference(patch_rows, source_embed, cell_embed, level_query, margin_rows, margin_counts, query_weight, key_weight, value_weight, out_weight, conv_weight):
    rows = patch_rows.reshape(PEERS, SOURCES, SRC_ROWS, D).astype(jnp.float32) + source_embed.astype(jnp.float32)[None, :, None, :]
    rows = rows.astype(jnp.bfloat16).reshape(ROWS_ALL, D)
    keys_all = jnp.dot(rows, key_weight, preferred_element_type=jnp.float32).astype(jnp.bfloat16).reshape(PEERS, P_DEV, D)
    vals_all = jnp.dot(rows, value_weight, preferred_element_type=jnp.float32).astype(jnp.bfloat16).reshape(PEERS, P_DEV, D)
    tiles = cell_embed.reshape(N_LON, LLON, N_LAT, LLAT, D).transpose(0, 2, 1, 3, 4).reshape(PEERS, LLON, LLAT, D)
    offsets = jnp.arange(3, dtype=jnp.int32) - 1
    flipped = (2 - jnp.arange(3, dtype=jnp.int32)).astype(jnp.int32)
    slots = jnp.arange(CAP, dtype=jnp.int32)

    def one_owner(operands):
        owner, tile = operands
        owner_lon = owner // N_LAT
        owner_lat = owner % N_LAT
        src_lon = (owner_lon + offsets[:, None]) % N_LON
        src_lat = jnp.clip(owner_lat + offsets[None, :], 0, N_LAT - 1)
        sources = (src_lon * N_LAT + src_lat).astype(jnp.int32)
        index = margin_rows[sources, flipped[:, None], flipped[None, :]]
        keys = keys_all[sources[:, :, None], index].reshape(9 * CAP, D)
        vals = vals_all[sources[:, :, None], index].reshape(9 * CAP, D)
        counts = margin_counts[owner]
        valid = (slots[None, None, :] < counts[:, :, None]).reshape(9 * CAP)
        latent_in = (tile[:, :, None, :].astype(jnp.float32) + level_query.astype(jnp.float32)[None, None]).astype(jnp.bfloat16)
        latent_in = latent_in.reshape(LLON * LLAT * LEVELS, D)
        return attend(latent_in, keys, vals, valid, query_weight, out_weight).reshape(LLON, LLAT, LEVELS, D)
    owned = lax.map(one_owner, (jnp.arange(PEERS, dtype=jnp.int32), tiles))
    state = owned.reshape(N_LON, N_LAT, LLON, LLAT, LEVELS, D).transpose(0, 2, 1, 3, 4, 5).reshape(NLON, NLAT, LEVELS, D)
    phi = (jnp.arange(NLAT, dtype=jnp.float32) + 0.5) / NLAT * jnp.pi - jnp.pi / 2
    cos_gain = 0.5 + jnp.cos(phi)
    for layer in range(LAYERS):
        scaled = normalize(state, cos_gain)
        top = jnp.roll(scaled[:, 0], -(NLON // 2), axis=0)
        bottom = jnp.roll(scaled[:, -1], -(NLON // 2), axis=0)
        padded = jnp.concatenate([top[:, None], scaled, bottom[:, None]], axis=1)
        padded = jnp.concatenate([padded[-1:], padded, padded[:1]], axis=0)
        conv = conv_taps(padded, conv_weight[layer], NLON, NLAT)
        state = (state.astype(jnp.float32) + jax.nn.gelu(conv, approximate=False)).astype(jnp.bfloat16)
    return state
```

```python
import functools
import math

import jax
import jax.numpy as jnp
from jax import lax
from jax.experimental import pallas as pl
from jax.experimental.pallas import tpu as pltpu
from jax.sharding import PartitionSpec as P

D = 512
HEADS = 16
HEAD = 32
CAP = 128
LON = 16
LAT = 32
CELLS = LON * LAT
LEVELS = 4
KEYS = 9 * CAP
SCALE = 1.0 / math.sqrt(HEAD)
LOG2E = 1.4426950408889634
CALM = 90.0
F32 = jnp.float32
BF16 = jnp.bfloat16
MIB = 1024 * 1024
NT = (((1,), (1,)), ((), ()))
TN = (((0,), (0,)), ((), ()))
AXES = ("lon", "lat")


def dot(a, b, dims=(((1,), (0,)), ((), ()))):
    return lax.dot_general(a, b, dims, preferred_element_type=F32)


def iota(shape, dim):
    return lax.broadcasted_iota(jnp.int32, shape, dim)


def gather_kernel(lat_ref, rows_ref, embed_ref, index_ref, out_ref, held):
    odd = lax.rem(lat_ref[0], 2)
    for s in range(4):
        part = rows_ref[s * 512 : (s + 1) * 512, :].astype(F32)
        held[s * 512 : (s + 1) * 512, :] = (part + embed_ref[s : s + 1, :].astype(F32)).astype(BF16)
    lanes = iota((CAP, 2048), 1)
    for a in range(3):
        picks = []
        for slot in range(3):
            if slot == 2:
                want = index_ref[0, a, 1:2, :]
            else:
                low, high = index_ref[0, a, 0:1, :], index_ref[0, a, 2:3, :]
                even_pick, odd_pick = (high, low) if slot == 0 else (low, high)
                want = jnp.where(odd == 1, odd_pick, even_pick)
            column = jnp.broadcast_to(want, (CAP, CAP)).T[:, 0:1]
            picks.append((lanes == column).astype(F32).astype(BF16))
        onehot = jnp.concatenate(picks, axis=0)
        out_ref[a] = dot(onehot, held[...]).astype(BF16).reshape(3, CAP, D)


def gather(lat, patch_rows, source_embed, margin_rows):
    return pl.pallas_call(
        gather_kernel,
        out_shape=jax.ShapeDtypeStruct((3, 3, CAP, D), BF16),
        in_specs=[
            pl.BlockSpec(memory_space=pltpu.SMEM),
            pl.BlockSpec(memory_space=pltpu.VMEM),
            pl.BlockSpec(memory_space=pltpu.VMEM),
            pl.BlockSpec(memory_space=pltpu.VMEM),
        ],
        out_specs=pl.BlockSpec(memory_space=pltpu.VMEM),
        scratch_shapes=[pltpu.VMEM((2048, D), BF16)],
        compiler_params=pltpu.CompilerParams(vmem_limit_bytes=40 * MIB),
        name="gather_rows",
    )(lat, patch_rows, source_embed, margin_rows)


def gain_of(lat, shape, dim):
    row = (lat * LAT + iota(shape, dim)).astype(F32)
    phi = (row + 0.5) / 128 * jnp.pi - jnp.pi / 2
    return 0.5 + jnp.cos(phi)


def normal(x, gain):
    spread = jnp.sqrt(jnp.mean(x * x, axis=-1, keepdims=True) + 1e-06)
    return x / spread * gain


def attend_kernel(
    lat_ref, count_ref, a0, a1, a2, a3, a4, a5, a6, a7, a8,
    cell_ref, level_ref, wq_ref, wk_ref, wv_ref, wo_ref,
    x_ref, k_s, v_s, q_s, att, live_col, live_row, ql_s,
):
    lists = (a0, a1, a2, a3, a4, a5, a6, a7, a8)
    for n, ref in enumerate(lists):
        span = slice(n * CAP, (n + 1) * CAP)
        rows = ref[...].reshape(CAP, D)
        k_s[span, :] = dot(rows, wk_ref[...]).astype(BF16)
        v_s[span, :] = dot(rows, wv_ref[...]).astype(BF16)
        live_col[span, :] = (iota((CAP, 128), 0) < count_ref[n]).astype(F32)
        live_row[:, span] = (iota((8, CAP), 1) < count_ref[n]).astype(F32)
    cells = cell_ref[...]
    level = jnp.concatenate([level_ref[...], level_ref[...]], axis=0)
    factor = SCALE * LOG2E
    qc = dot(cells, wq_ref[...]) * factor
    ql = dot(level, wq_ref[...]) * factor
    q_s[...] = qc.astype(BF16)
    ql_s[...] = ql
    heads = (iota((D, 128), 0) // HEAD == iota((D, 128), 1)).astype(F32).astype(BF16)

    def norms(values):
        return jnp.max(dot((values * values).astype(BF16), heads), axis=0, keepdims=True)

    keys_f = k_s[...].astype(F32)
    key_norm = norms(keys_f)
    bound = jnp.sqrt(norms(qc) * key_norm) + jnp.sqrt(norms(ql) * key_norm)
    calm = jnp.max(bound) < CALM
    group_lane = iota((1, 128), 1) // HEAD

    @pl.when(calm)
    def _():
        def group(hg, carry):
            lanes = pl.ds(pl.multiple_of(hg * 128, 128), 128)
            kg = k_s[:, lanes]
            vg = v_s[:, lanes]
            qg = q_s[:, lanes]
            lg = ql_s[:, lanes].astype(BF16)
            col = iota((8, 512), 1)
            pick = (col // HEAD % 4 - col // 128 + 4) % 4
            choose = ((iota((8, 512), 0) == pick) & (iota((8, 512), 0) < 4)).astype(F32).astype(BF16)
            spread = dot(lg, choose, TN)
            col2, row2 = iota((128, 512), 1), iota((128, 512), 0)
            own = row2 // HEAD == col2 // 128
            ql_block = jnp.where(own, spread, 0.0).astype(BF16)
            copies = (own & (row2 % HEAD == col2 % HEAD)).astype(F32).astype(BF16)
            level_exp = jnp.exp2(dot(kg, ql_block))
            vals = dot(vg, copies)
            live = live_col[...]
            kept = []
            for i in range(4):
                span = slice(i * 128, (i + 1) * 128)
                part = level_exp[:, span] * live
                weighted = jnp.concatenate([part * vals[:, span], part], axis=1).astype(BF16)
                km = jnp.where(group_lane == i, kg, jnp.zeros_like(kg))
                probs = jnp.exp2(dot(qg, km, NT)).astype(BF16)
                both = dot(probs, weighted)
                kept.append(both[:, :128] / both[:, 128:])
            for lev in range(LEVELS):
                z = kept[0]
                for i in range(4):
                    z = jnp.where(group_lane == (i + lev) % 4, kept[i], z)
                if lev:
                    z = pltpu.roll(z, 128 - HEAD * lev, axis=1)
                att[lev, :, lanes] = z.astype(BF16)
            return carry

        lax.fori_loop(0, 4, group, 0)

    @pl.when(jnp.logical_not(calm))
    def _():
        def one_level(lev, carry):
            four = level_ref[...].astype(F32)
            mine = jnp.sum(jnp.where(iota((LEVELS, D), 0) == lev, four, 0.0), axis=0, keepdims=True)
            latent = (cell_ref[...].astype(F32) + mine).astype(BF16)
            q_s[...] = dot(latent, wq_ref[...]).astype(BF16)

            def group(hg, carry):
                lanes = pl.ds(pl.multiple_of(hg * 128, 128), 128)
                kg = k_s[:, lanes]
                vg = v_s[:, lanes]
                qg = q_s[:, lanes]

                def head(i, total):
                    mine = group_lane == i
                    scores = dot(qg, jnp.where(mine, kg, jnp.zeros_like(kg)), NT) * SCALE
                    scores = jnp.where(live_row[0:1, :] > 0.5, scores, -1e30)
                    top = jnp.max(scores, axis=1, keepdims=True)
                    weights = jnp.exp(scores - top)
                    probs = (weights / jnp.sum(weights, axis=1, keepdims=True)).astype(BF16)
                    return total + dot(probs, jnp.where(mine, vg, jnp.zeros_like(vg)))

                total = lax.fori_loop(0, 4, head, jnp.zeros((CELLS, 128), F32))
                att[lev, :, lanes] = total.astype(BF16)
                return carry

            return lax.fori_loop(0, 4, group, carry)

        lax.fori_loop(0, LEVELS, one_level, 0)

    for lev in range(LEVELS):
        latent = (cell_ref[...].astype(F32) + level_ref[lev : lev + 1, :].astype(F32)).astype(BF16)
        x = (latent.astype(F32) + dot(att[lev], wo_ref[...])).astype(BF16)
        x_ref[lev] = x


def attend(lat, counts, lists, cells, level_query, wq, wk, wv, wo):
    vmem = pl.BlockSpec(memory_space=pltpu.VMEM)
    smem = pl.BlockSpec(memory_space=pltpu.SMEM)
    return pl.pallas_call(
        attend_kernel,
        out_shape=jax.ShapeDtypeStruct((LEVELS, CELLS, D), BF16),
        in_specs=[smem, smem] + [vmem] * 15,
        out_specs=vmem,
        scratch_shapes=[
            pltpu.VMEM((KEYS, D), BF16),
            pltpu.VMEM((KEYS, D), BF16),
            pltpu.VMEM((CELLS, D), BF16),
            pltpu.VMEM((LEVELS, CELLS, D), BF16),
            pltpu.VMEM((KEYS, 128), F32),
            pltpu.VMEM((8, KEYS), F32),
            pltpu.VMEM((8, D), F32),
        ],
        compiler_params=pltpu.CompilerParams(vmem_limit_bytes=56 * MIB),
        name="attend",
    )(lat, counts, *lists, cells, level_query, wq, wk, wv, wo)


def conv_kernel(lat_ref, x_ref, west_ref, east_ref, north_ref, south_ref, w_ref, out_ref, near):
    gain = gain_of(lat_ref[0], (LAT, D), 0)
    x = x_ref[0].astype(F32)
    u = normal(x, jnp.tile(gain, (LON, 1))).astype(BF16).astype(F32)
    wide = jnp.concatenate([west_ref[0].astype(F32), u, east_ref[0].astype(F32)], axis=0)
    count = (LON + 2) * LAT
    place = iota((LON + 2, LAT, D), 1)
    before = pltpu.roll(wide, 1, axis=0).reshape(LON + 2, LAT, D)
    after = pltpu.roll(wide, count - 1, axis=0).reshape(LON + 2, LAT, D)
    north = north_ref[0].astype(F32)[:, None, :]
    south = south_ref[0].astype(F32)[:, None, :]
    near[:, 0:512] = jnp.where(place == 0, north, before).astype(BF16).reshape(count, D)
    near[:, 512:1024] = wide.astype(BF16)
    near[:, 1024:1536] = jnp.where(place == LAT - 1, south, after).astype(BF16).reshape(count, D)
    total = dot(near[0:CELLS, :], w_ref[0])
    total += dot(near[LAT : LAT + CELLS, :], w_ref[1])
    total += dot(near[2 * LAT : 2 * LAT + CELLS, :], w_ref[2])
    gelu = 0.5 * total * (1.0 + lax.erf(total * (2.0 ** -0.5)))
    out_ref[0] = (x + gelu).astype(BF16)


def conv(lat, x, west, east, north, south, weight):
    per = lambda rows: pl.BlockSpec((1, rows, D), lambda i: (i, 0, 0))
    return pl.pallas_call(
        conv_kernel,
        grid=(LEVELS,),
        out_shape=jax.ShapeDtypeStruct((LEVELS, CELLS, D), BF16),
        in_specs=[
            pl.BlockSpec(memory_space=pltpu.SMEM),
            per(CELLS), per(LAT), per(LAT), per(LON + 2), per(LON + 2),
            pl.BlockSpec((3, 3 * D, D), lambda i: (0, 0, 0)),
        ],
        out_specs=per(CELLS),
        scratch_shapes=[pltpu.VMEM(((LON + 2) * LAT, 3 * D), BF16)],
        compiler_params=pltpu.CompilerParams(vmem_limit_bytes=56 * MIB),
        name="conv",
    )(lat, x, west, east, north, south, weight)


def route(target):
    pairs = []
    for lon in range(32):
        for lat in range(4):
            there = target(lon, lat)
            if there is not None:
                pairs.append((lon * 4 + lat, there[0] % 32 * 4 + there[1]))
    return pairs


EAST = route(lambda lon, lat: (lon + 1, lat))
WEST = route(lambda lon, lat: (lon - 1, lat))
FIRST = route(lambda lon, lat: (lon, lat ^ 1))
SECOND = route(lambda lon, lat: (lon + 16 if lat in (0, 3) else lon, (0, 2, 1, 3)[lat]))


def send(block, pairs):
    return lax.ppermute(block, AXES, pairs)


def edges(x, lat, lat_place):
    grid = x.reshape(LEVELS, LON, LAT, D)
    gain = 0.5 + jnp.cos((lat_place * LAT + jnp.arange(LAT)).astype(F32) * (jnp.pi / 128) + (0.5 * jnp.pi / 128 - jnp.pi / 2))

    def u(part, scale):
        return normal(part.astype(F32), scale).astype(BF16)

    first = u(grid[:, 0], gain[:, None])
    last = u(grid[:, LON - 1], gain[:, None])
    north = u(grid[:, :, 0], gain[0])
    south = u(grid[:, :, LAT - 1], gain[LAT - 1])
    return first, last, north, south


def halos(x, lat, lat_place):
    first, last, north, south = edges(x, lat, lat_place)
    west = send(last, EAST)
    east = send(first, WEST)
    north = jnp.concatenate([west[:, :1], north, east[:, :1]], axis=1)
    south = jnp.concatenate([west[:, -1:], south, east[:, -1:]], axis=1)
    odd = lat_place % 2 == 1
    one = send(jnp.where(odd, north, south), FIRST)
    two = send(jnp.where(odd, south, north), SECOND)
    return west, east, jnp.where(odd, one, two), jnp.where(odd, two, one)


def shards(
    patch_rows, source_embed, cell_embed, level_query, margin_rows, margin_counts,
    query_weight, key_weight, value_weight, out_weight, conv_weight,
):
    lat_place = lax.axis_index("lat")
    lat = lat_place.astype(jnp.int32).reshape(1)
    payload = gather(lat, patch_rows, source_embed, margin_rows)
    from_west = send(payload[2], EAST)
    from_east = send(payload[0], WEST)
    own = payload[1]
    one = send(jnp.stack([from_west[0], own[0], from_east[0]]), FIRST)
    two = send(jnp.stack([from_west[1], own[1], from_east[1]]), SECOND)
    lists = [from_west[2], own[2], from_east[2], one[0], one[1], one[2], two[0], two[1], two[2]]
    odd = lat_place % 2 == 1
    counts = margin_counts[0]
    first = jnp.where(odd, counts[:, 0], counts[:, 2])
    second = jnp.where(odd, counts[:, 2], counts[:, 0])
    counts = jnp.concatenate([counts[:, 1], first, second])
    x = attend(lat, counts, lists, cell_embed.reshape(CELLS, D), level_query,
               query_weight, key_weight, value_weight, out_weight)
    weight = conv_weight.reshape(2, 3, 3 * D, D)
    for layer in range(2):
        west, east, north, south = halos(x, lat, lat_place)
        x = conv(lat, x, west, east, north, south, weight[layer])
    return x.reshape(LEVELS, LON, LAT, D).transpose(1, 2, 0, 3)


def solution(mesh):
    placed = (
        P(AXES, None), P(), P("lon", "lat", None), P(), P(AXES, None, None, None), P(AXES, None, None),
        P(), P(), P(), P(), P(),
    )
    return jax.shard_map(
        shards, mesh=mesh, in_specs=placed, out_specs=P("lon", "lat", None, None), check_vma=False
    )
```

```python
import functools
import math

import jax
import jax.numpy as jnp
from jax import lax
from jax.experimental import pallas as pl
from jax.experimental.pallas import tpu as pltpu
from jax.sharding import PartitionSpec as P

D = 512
HEADS = 16
HEAD = 32
CAP = 128
LON = 16
LAT = 32
CELLS = LON * LAT
LEVELS = 4
KEYS = 9 * CAP
SCALE = 1.0 / math.sqrt(HEAD)
LOG2E = 1.4426950408889634
CALM = 90.0
F32 = jnp.float32
BF16 = jnp.bfloat16
MIB = 1024 * 1024
NT = (((1,), (1,)), ((), ()))
TN = (((0,), (0,)), ((), ()))
AXES = ("lon", "lat")


def dot(a, b, dims=(((1,), (0,)), ((), ()))):
    return lax.dot_general(a, b, dims, preferred_element_type=F32)


def iota(shape, dim):
    return lax.broadcasted_iota(jnp.int32, shape, dim)


def gather_kernel(lat_ref, rows_ref, embed_ref, index_ref, out_ref, held):
    odd = lax.rem(lat_ref[0], 2)
    for s in range(4):
        part = rows_ref[s * 512 : (s + 1) * 512, :].astype(F32)
        held[s * 512 : (s + 1) * 512, :] = (part + embed_ref[s : s + 1, :].astype(F32)).astype(BF16)
    lanes = iota((CAP, 2048), 1)
    for a in range(3):
        picks = []
        for slot in range(3):
            if slot == 2:
                want = index_ref[0, a, 1:2, :]
            else:
                low, high = index_ref[0, a, 0:1, :], index_ref[0, a, 2:3, :]
                even_pick, odd_pick = (high, low) if slot == 0 else (low, high)
                want = jnp.where(odd == 1, odd_pick, even_pick)
            column = jnp.broadcast_to(want, (CAP, CAP)).T[:, 0:1]
            picks.append((lanes == column).astype(F32).astype(BF16))
        onehot = jnp.concatenate(picks, axis=0)
        out_ref[a] = dot(onehot, held[...]).astype(BF16).reshape(3, CAP, D)


def gather(lat, patch_rows, source_embed, margin_rows):
    return pl.pallas_call(
        gather_kernel,
        out_shape=jax.ShapeDtypeStruct((3, 3, CAP, D), BF16),
        in_specs=[
            pl.BlockSpec(memory_space=pltpu.SMEM),
            pl.BlockSpec(memory_space=pltpu.VMEM),
            pl.BlockSpec(memory_space=pltpu.VMEM),
            pl.BlockSpec(memory_space=pltpu.VMEM),
        ],
        out_specs=pl.BlockSpec(memory_space=pltpu.VMEM),
        scratch_shapes=[pltpu.VMEM((2048, D), BF16)],
        compiler_params=pltpu.CompilerParams(vmem_limit_bytes=40 * MIB),
        name="gather_rows",
    )(lat, patch_rows, source_embed, margin_rows)


def gain_of(lat, shape, dim):
    row = (lat * LAT + iota(shape, dim)).astype(F32)
    phi = (row + 0.5) / 128 * jnp.pi - jnp.pi / 2
    return 0.5 + jnp.cos(phi)


def normal(x, gain):
    spread = jnp.sqrt(jnp.mean(x * x, axis=-1, keepdims=True) + 1e-06)
    return x / spread * gain


def edge_pick():
    row, col = iota((2 * LON, CELLS), 0), iota((2 * LON, CELLS), 1)
    return (col == row % LON * LAT + row // LON * (LAT - 1)).astype(F32).astype(BF16)


def pair_rows(lat, lev, north, south, gain, one_ref, two_ref):
    north = normal(north, gain[0:1, :])
    south = normal(south, gain[LAT - 1 :, :])
    odd = lax.rem(lat, 2) == 1
    one_ref[lev] = jnp.where(odd, north, south).astype(BF16)
    two_ref[lev] = jnp.where(odd, south, north).astype(BF16)


def attend_kernel(
    lat_ref, count_ref, a0, a1, a2, a3, a4, a5, a6, a7, a8,
    cell_ref, level_ref, wq_ref, wk_ref, wv_ref, wo_ref,
    x_ref, west_ref, east_ref, one_ref, two_ref, k_s, v_s, q_s, att, live_col, live_row, ql_s,
):
    lists = (a0, a1, a2, a3, a4, a5, a6, a7, a8)
    for n, ref in enumerate(lists):
        span = slice(n * CAP, (n + 1) * CAP)
        rows = ref[...].reshape(CAP, D)
        k_s[span, :] = dot(rows, wk_ref[...]).astype(BF16)
        v_s[span, :] = dot(rows, wv_ref[...]).astype(BF16)
        live_col[span, :] = (iota((CAP, 128), 0) < count_ref[n]).astype(F32)
        live_row[:, span] = (iota((8, CAP), 1) < count_ref[n]).astype(F32)
    cells = cell_ref[...]
    level = jnp.concatenate([level_ref[...], level_ref[...]], axis=0)
    factor = SCALE * LOG2E
    qc = dot(cells, wq_ref[...]) * factor
    ql = dot(level, wq_ref[...]) * factor
    q_s[...] = qc.astype(BF16)
    ql_s[...] = ql
    heads = (iota((D, 128), 0) // HEAD == iota((D, 128), 1)).astype(F32).astype(BF16)

    def norms(values):
        return jnp.max(dot((values * values).astype(BF16), heads), axis=0, keepdims=True)

    keys_f = k_s[...].astype(F32)
    key_norm = norms(keys_f)
    bound = jnp.sqrt(norms(qc) * key_norm) + jnp.sqrt(norms(ql) * key_norm)
    calm = jnp.max(bound) < CALM
    group_lane = iota((1, 128), 1) // HEAD

    @pl.when(calm)
    def _():
        def group(hg, carry):
            lanes = pl.ds(pl.multiple_of(hg * 128, 128), 128)
            kg = k_s[:, lanes]
            vg = v_s[:, lanes]
            qg = q_s[:, lanes]
            lg = ql_s[:, lanes].astype(BF16)
            col = iota((8, 512), 1)
            pick = (col // HEAD % 4 - col // 128 + 4) % 4
            choose = ((iota((8, 512), 0) == pick) & (iota((8, 512), 0) < 4)).astype(F32).astype(BF16)
            spread = dot(lg, choose, TN)
            col2, row2 = iota((128, 512), 1), iota((128, 512), 0)
            own = row2 // HEAD == col2 // 128
            ql_block = jnp.where(own, spread, 0.0).astype(BF16)
            copies = (own & (row2 % HEAD == col2 % HEAD)).astype(F32).astype(BF16)
            level_exp = jnp.exp2(dot(kg, ql_block))
            vals = dot(vg, copies)
            live = live_col[...]
            kept = []
            for i in range(4):
                span = slice(i * 128, (i + 1) * 128)
                part = level_exp[:, span] * live
                weighted = jnp.concatenate([part * vals[:, span], part], axis=1).astype(BF16)
                km = jnp.where(group_lane == i, kg, jnp.zeros_like(kg))
                probs = jnp.exp2(dot(qg, km, NT)).astype(BF16)
                both = dot(probs, weighted)
                kept.append(both[:, :128] / both[:, 128:])
            for lev in range(LEVELS):
                z = kept[0]
                for i in range(4):
                    z = jnp.where(group_lane == (i + lev) % 4, kept[i], z)
                if lev:
                    z = pltpu.roll(z, 128 - HEAD * lev, axis=1)
                att[lev, :, lanes] = z.astype(BF16)
            return carry

        lax.fori_loop(0, 4, group, 0)

    @pl.when(jnp.logical_not(calm))
    def _():
        def one_level(lev, carry):
            four = level_ref[...].astype(F32)
            mine = jnp.sum(jnp.where(iota((LEVELS, D), 0) == lev, four, 0.0), axis=0, keepdims=True)
            latent = (cell_ref[...].astype(F32) + mine).astype(BF16)
            q_s[...] = dot(latent, wq_ref[...]).astype(BF16)

            def group(hg, carry):
                lanes = pl.ds(pl.multiple_of(hg * 128, 128), 128)
                kg = k_s[:, lanes]
                vg = v_s[:, lanes]
                qg = q_s[:, lanes]

                def head(i, total):
                    mine = group_lane == i
                    scores = dot(qg, jnp.where(mine, kg, jnp.zeros_like(kg)), NT) * SCALE
                    scores = jnp.where(live_row[0:1, :] > 0.5, scores, -1e30)
                    top = jnp.max(scores, axis=1, keepdims=True)
                    weights = jnp.exp(scores - top)
                    probs = (weights / jnp.sum(weights, axis=1, keepdims=True)).astype(BF16)
                    return total + dot(probs, jnp.where(mine, vg, jnp.zeros_like(vg)))

                total = lax.fori_loop(0, 4, head, jnp.zeros((CELLS, 128), F32))
                att[lev, :, lanes] = total.astype(BF16)
                return carry

            return lax.fori_loop(0, 4, group, carry)

        lax.fori_loop(0, LEVELS, one_level, 0)

    for lev in range(LEVELS):
        latent = (cell_ref[...].astype(F32) + level_ref[lev : lev + 1, :].astype(F32)).astype(BF16)
        x = (latent.astype(F32) + dot(att[lev], wo_ref[...])).astype(BF16)
        x_ref[lev] = x
        edge_rows = dot(edge_pick(), x)
        gain = gain_of(lat_ref[0], (LAT, D), 0)
        west_ref[lev] = normal(x[:LAT, :].astype(F32), gain).astype(BF16)
        east_ref[lev] = normal(x[CELLS - LAT :, :].astype(F32), gain).astype(BF16)
        pair_rows(lat_ref[0], lev, edge_rows[:LON], edge_rows[LON:], gain, one_ref, two_ref)


def attend(lat, counts, lists, cells, level_query, wq, wk, wv, wo):
    vmem = pl.BlockSpec(memory_space=pltpu.VMEM)
    smem = pl.BlockSpec(memory_space=pltpu.SMEM)
    return pl.pallas_call(
        attend_kernel,
        out_shape=(
            jax.ShapeDtypeStruct((LEVELS, CELLS, D), BF16),
            jax.ShapeDtypeStruct((LEVELS, LAT, D), BF16),
            jax.ShapeDtypeStruct((LEVELS, LAT, D), BF16),
            jax.ShapeDtypeStruct((LEVELS, LON, D), BF16),
            jax.ShapeDtypeStruct((LEVELS, LON, D), BF16),
        ),
        in_specs=[smem, smem] + [vmem] * 15,
        out_specs=(vmem,) * 5,
        scratch_shapes=[
            pltpu.VMEM((KEYS, D), BF16),
            pltpu.VMEM((KEYS, D), BF16),
            pltpu.VMEM((CELLS, D), BF16),
            pltpu.VMEM((LEVELS, CELLS, D), BF16),
            pltpu.VMEM((KEYS, 128), F32),
            pltpu.VMEM((8, KEYS), F32),
            pltpu.VMEM((8, D), F32),
        ],
        compiler_params=pltpu.CompilerParams(vmem_limit_bytes=56 * MIB),
        name="attend",
    )(lat, counts, *lists, cells, level_query, wq, wk, wv, wo)


def fetch_weights(layer, w_hbm, w_s, sems):
    for a in range(3):
        pltpu.make_async_copy(w_hbm.at[layer, a], w_s.at[a], sems.at[a]).start()


def wait_weights(layer, a, w_hbm, w_s, sems):
    pltpu.make_async_copy(w_hbm.at[layer, a], w_s.at[a], sems.at[a]).wait()


def gelu(total):
    return 0.5 * total * (1.0 + lax.erf(total * (2.0 ** -0.5)))


def read_x(x_refs, lev, low, high):
    if len(x_refs) == 1:
        return x_refs[0][lev, low * LAT : high * LAT, :].astype(F32)
    inner, outer, rim = x_refs
    parts = []
    for lon in range(low, high):
        if 4 <= lon < 12:
            part = inner[lev, (lon - 4) * LAT : (lon - 3) * LAT, :]
        else:
            place = lon if lon < 4 else lon - 8
            part = outer[lev, place * LAT : (place + 1) * LAT, :]
        parts.append(part.astype(F32))
    rows = jnp.concatenate(parts, axis=0).reshape(high - low, LAT, D)
    edge = rim[lev].astype(F32)
    place = iota((high - low, LAT, D), 1)
    rows = jnp.where(place == 0, edge[low:high][:, None, :], rows)
    rows = jnp.where(place == LAT - 1, edge[LON + low : LON + high][:, None, :], rows)
    return rows.reshape((high - low) * LAT, D)


def three_shifts(near, wide):
    count = wide.shape[0]
    row = iota((count, D), 0) % LAT
    near[:, 0:D] = jnp.where(row == 0, 0.0, pltpu.roll(wide, 1, axis=0)).astype(BF16)
    near[:, D : 2 * D] = wide.astype(BF16)
    near[:, 2 * D :] = jnp.where(row == LAT - 1, 0.0, pltpu.roll(wide, count - 1, axis=0)).astype(BF16)


def inner_kernel(layer, parts, lat_ref, *refs):
    x_refs, (w_hbm, out_ref), (near, w_s, sems), stage = refs[:parts], refs[parts : parts + 2], refs[parts + 2 : parts + 5], refs[parts + 5 :]
    fetch_weights(layer, w_hbm, w_s, sems)
    gain = gain_of(lat_ref[0], (LAT, D), 0)
    gains = jnp.concatenate([gain] * 10, axis=0)
    for lev in range(LEVELS):
        wide = normal(read_x(x_refs, lev, 3, 13), gains).astype(BF16).astype(F32)
        three_shifts(near.at[lev], wide)
    for a in range(3):
        wait_weights(layer, a, w_hbm, w_s, sems)
    for lev in range(0, LEVELS, 2):
        total = None
        for a in range(3):
            window = near[lev : lev + 2, a * LAT : a * LAT + 256, :].reshape(512, 3 * D)
            part = dot(window, w_s[a])
            total = part if total is None else total + part
        moved = gelu(total)
        for k in range(2):
            y = (read_x(x_refs[:1] if parts == 1 else x_refs, lev + k, 4, 12) + moved[k * 256 : (k + 1) * 256]).astype(BF16)
            if stage:
                stage[0][:, lev + k, :] = y
            else:
                out_ref[lev + k] = y
    if stage:
        copy = pltpu.make_async_copy(stage[0], out_ref.at[pl.ds(128, 256)], stage[1].at[0])
        copy.start()
        copy.wait()


def outer_kernel(layer, parts, lat_ref, *refs):
    x_refs, refs = refs[:parts], refs[parts:]
    if layer:
        west_ref, east_ref, w_hbm, _, _, out_ref, near, w_s, sems = refs[:9]
        stage = refs[9:]
    else:
        west_ref, east_ref, w_hbm, _, out_ref, near, w_s, sems = refs[:8]
        stage = ()
    fetch_weights(layer, w_hbm, w_s, sems)
    gain = gain_of(lat_ref[0], (LAT, D), 0)
    gains = jnp.concatenate([gain] * 5, axis=0)
    for lev in range(LEVELS):
        low = normal(read_x(x_refs, lev, 0, 5), gains).astype(BF16).astype(F32)
        three_shifts(near.at[lev, 0], jnp.concatenate([west_ref[lev].astype(F32), low], axis=0))
        high = normal(read_x(x_refs, lev, 11, 16), gains).astype(BF16).astype(F32)
        three_shifts(near.at[lev, 1], jnp.concatenate([high, east_ref[lev].astype(F32)], axis=0))
    for a in range(3):
        wait_weights(layer, a, w_hbm, w_s, sems)
    for lev in range(0, LEVELS, 2):
        total = None
        for a in range(3):
            window = near[lev : lev + 2, :, a * LAT : a * LAT + 128, :].reshape(512, 3 * D)
            part = dot(window, w_s[a])
            total = part if total is None else total + part
        moved = gelu(total)
        for k in range(2):
            old = jnp.concatenate([read_x(x_refs, lev + k, 0, 4), read_x(x_refs, lev + k, 12, 16)], axis=0)
            y = (old + moved[k * 256 : (k + 1) * 256]).astype(BF16)
            if stage:
                stage[0][:, lev + k, :] = y
            else:
                out_ref[lev + k] = y
    if stage:
        copies = [
            pltpu.make_async_copy(stage[0].at[pl.ds(0, 128)], out_ref.at[pl.ds(0, 128)], stage[1].at[0]),
            pltpu.make_async_copy(stage[0].at[pl.ds(128, 128)], out_ref.at[pl.ds(384, 128)], stage[1].at[1]),
        ]
        for copy in copies:
            copy.start()
        for copy in copies:
            copy.wait()


def rim_kernel(layer, parts, lat_ref, *refs):
    x_refs, refs = refs[:parts], refs[parts:]
    west_ref, east_ref, one_ref, two_ref, w_hbm = refs[:5]
    refs = refs[5:]
    if layer:
        _, out_ref, taps, w_s, sems, stage, stage_sems = refs
    else:
        outer_ref, rim_ref, west_out, east_out, one_out, two_out, taps, w_s, sems = refs
    fetch_weights(layer, w_hbm, w_s, sems)
    lat = lat_ref[0]
    odd = lax.rem(lat, 2) == 1
    gain = gain_of(lat, (LAT, D), 0)
    lon = iota((LON, D), 0)
    old = []
    for lev in range(LEVELS):
        row, col = iota((4 * LON, CELLS), 0), iota((4 * LON, CELLS), 1)
        lat_row = jnp.where(row < 2 * LON, row // LON, row // LON + LAT - 4)
        if parts == 1:
            pick = (col == row % LON * LAT + lat_row).astype(F32).astype(BF16)
            four = dot(pick, x_refs[0][lev])
        else:
            inner, outer, rim = x_refs
            spot = (row % LON + 12) % LON
            spot = jnp.where(spot < 8, spot, jnp.where(spot >= 12, spot - 4, spot + 4))
            pick = (col == spot * LAT + lat_row).astype(F32).astype(BF16)
            four = dot(pick[:, :256], inner[lev]) + dot(pick[:, 256:], outer[lev])
        rows = [four[n * LON : (n + 1) * LON] for n in range(4)]
        if parts > 1:
            rows[0] = rim[lev, 0:LON, :].astype(F32)
            rows[3] = rim[lev, LON:, :].astype(F32)
        old.append((rows[0], rows[3]))
        one, two = one_ref[lev].astype(F32), two_ref[lev].astype(F32)
        north = jnp.where(odd, one, two)
        south = jnp.where(odd, two, one)
        shifted = []
        for place, x in zip((0, 1, LAT - 2, LAT - 1), rows):
            u = normal(x, gain[place : place + 1, :]).astype(BF16).astype(F32)
            west = west_ref[lev, place : place + 1, :].astype(F32)
            east = east_ref[lev, place : place + 1, :].astype(F32)
            shifted.append((
                jnp.where(lon == 0, west, pltpu.roll(u, 1, axis=0)),
                u,
                jnp.where(lon == LON - 1, east, pltpu.roll(u, LON - 1, axis=0)),
            ))
        for a in range(3):
            top = jnp.concatenate([north[a : a + LON], shifted[0][a], shifted[1][a]], axis=1)
            low = jnp.concatenate([shifted[2][a], shifted[3][a], south[a : a + LON]], axis=1)
            taps[a, lev * 32 : lev * 32 + 16, :] = top.astype(BF16)
            taps[a, lev * 32 + 16 : lev * 32 + 32, :] = low.astype(BF16)
    total = None
    for a in range(3):
        wait_weights(layer, a, w_hbm, w_s, sems)
        part = dot(taps[a], w_s[a])
        total = part if total is None else total + part
    moved = gelu(total)
    copies = []
    for lev in range(LEVELS):
        top = (old[lev][0] + moved[lev * 32 : lev * 32 + 16]).astype(BF16)
        low = (old[lev][1] + moved[lev * 32 + 16 : lev * 32 + 32]).astype(BF16)
        if layer:
            stage[0:LON, lev, :] = top
            stage[LON:, lev, :] = low
            continue
        rim_ref[lev, 0:LON, :] = top
        rim_ref[lev, LON:, :] = low
        top, low = top.astype(F32), low.astype(F32)
        pair_rows(lat, lev, top, low, gain, one_out, two_out)
        place = iota((LAT, D), 0)
        for ref, start, k in ((west_out, 0, 0), (east_out, 7 * LAT, LON - 1)):
            column = outer_ref[lev, start : start + LAT, :].astype(F32)
            column = jnp.where(place == 0, top[k : k + 1], column)
            column = jnp.where(place == LAT - 1, low[k : k + 1], column)
            ref[lev] = normal(column, gain).astype(BF16)
    if layer:
        for k in range(LON):
            for side in range(2):
                copies.append(pltpu.make_async_copy(
                    stage.at[side * LON + k], out_ref.at[k * LAT + side * (LAT - 1)], stage_sems.at[side * LON + k]
                ))
        for copy in copies:
            copy.start()
        for copy in copies:
            copy.wait()


def conv_call(kernel, layer, operands, out_shape, scratch, alias, rows, name):
    spaces = {"s": pltpu.SMEM, "v": pltpu.VMEM, "a": pl.ANY}
    whole = isinstance(out_shape, tuple)
    return pl.pallas_call(
        kernel,
        out_shape=out_shape,
        in_specs=[pl.BlockSpec(memory_space=spaces[kind]) for _, kind in operands],
        out_specs=tuple(pl.BlockSpec(memory_space=pltpu.VMEM) for _ in out_shape) if whole
        else pl.BlockSpec(memory_space=pl.ANY if layer else pltpu.VMEM),
        scratch_shapes=scratch,
        input_output_aliases=alias,
        compiler_params=pltpu.CompilerParams(vmem_limit_bytes=48 * MIB),
        cost_estimate=pl.CostEstimate(flops=rows * 9 * D * D * 2, bytes_accessed=8 * MIB, transcendentals=0),
        name=name,
    )(*[array for array, _ in operands])


def layer_step(layer, lat, lat_place, xs, west_u, east_u, one_u, two_u, weight):
    parts = len(xs)
    weights = [pltpu.VMEM((3, 3 * D, D), BF16), pltpu.SemaphoreType.DMA((3,))]
    state = [(x, "v") for x in xs]
    full = jax.ShapeDtypeStruct((CELLS, LEVELS, D), BF16)
    half = jax.ShapeDtypeStruct((LEVELS, CELLS // 2, D), BF16)
    stage = [pltpu.VMEM((256, LEVELS, D), BF16), pltpu.SemaphoreType.DMA((2,))] if layer else []
    west = send(east_u, EAST)
    east = send(west_u, WEST)
    inner = conv_call(
        functools.partial(inner_kernel, layer, parts), layer,
        [(lat, "s")] + state + [(weight, "a")], full if layer else half,
        [pltpu.VMEM((LEVELS, 10 * LAT, 3 * D), BF16)] + weights + stage, {}, 1024, "conv_inner",
    )
    odd = lat_place % 2 == 1

    def with_corners(middle, row_if_odd, row_if_even):
        left = jnp.where(odd, west[:, row_if_odd], west[:, row_if_even])
        right = jnp.where(odd, east[:, row_if_odd], east[:, row_if_even])
        return jnp.concatenate([left[:, None], middle, right[:, None]], axis=1)

    one_u = with_corners(one_u, 0, LAT - 1)
    two_u = with_corners(two_u, LAT - 1, 0)
    one = send(one_u, FIRST)
    two = send(two_u, SECOND)
    operands = [(lat, "s")] + state + [(west, "v"), (east, "v"), (weight, "a"), (one_u, "a")]
    if layer:
        operands.append((inner, "a"))
    outer = conv_call(
        functools.partial(outer_kernel, layer, parts), layer, operands, full if layer else half,
        [pltpu.VMEM((LEVELS, 2, 6 * LAT, 3 * D), BF16)] + weights + stage,
        {len(operands) - 1: 0} if layer else {}, 1024, "conv_outer",
    )
    operands = [(lat, "s")] + state + [(west, "v"), (east, "v"), (one, "v"), (two, "v"), (weight, "a")]
    operands.append((outer, "a" if layer else "v"))
    shapes = full if layer else tuple(
        jax.ShapeDtypeStruct((LEVELS, rows, D), BF16) for rows in (2 * LON, LAT, LAT, LON, LON)
    )
    done = conv_call(
        functools.partial(rim_kernel, layer, parts), layer, operands, shapes,
        [pltpu.VMEM((3, 128, 3 * D), BF16)] + weights
        + ([pltpu.VMEM((32, LEVELS, D), BF16), pltpu.SemaphoreType.DMA((32,))] if layer else []),
        {len(operands) - 1: 0} if layer else {}, 128, "conv_rim",
    )
    if layer:
        return done
    rim, west_u, east_u, one_u, two_u = done
    return (inner, outer, rim), west_u, east_u, one_u, two_u


def route(target):
    pairs = []
    for lon in range(32):
        for lat in range(4):
            there = target(lon, lat)
            if there is not None:
                pairs.append((lon * 4 + lat, there[0] % 32 * 4 + there[1]))
    return pairs


EAST = route(lambda lon, lat: (lon + 1, lat))
WEST = route(lambda lon, lat: (lon - 1, lat))
FIRST = route(lambda lon, lat: (lon, lat ^ 1))
SECOND = route(lambda lon, lat: (lon + 16 if lat in (0, 3) else lon, (0, 2, 1, 3)[lat]))


def send(block, pairs):
    return lax.ppermute(block, AXES, pairs)


def shards(
    patch_rows, source_embed, cell_embed, level_query, margin_rows, margin_counts,
    query_weight, key_weight, value_weight, out_weight, conv_weight,
):
    lat_place = lax.axis_index("lat")
    lat = lat_place.astype(jnp.int32).reshape(1)
    payload = gather(lat, patch_rows, source_embed, margin_rows)
    from_west = send(payload[2], EAST)
    from_east = send(payload[0], WEST)
    own = payload[1]
    one = send(jnp.stack([from_west[0], own[0], from_east[0]]), FIRST)
    two = send(jnp.stack([from_west[1], own[1], from_east[1]]), SECOND)
    lists = [from_west[2], own[2], from_east[2], one[0], one[1], one[2], two[0], two[1], two[2]]
    odd = lat_place % 2 == 1
    counts = margin_counts[0]
    first = jnp.where(odd, counts[:, 0], counts[:, 2])
    second = jnp.where(odd, counts[:, 2], counts[:, 0])
    counts = jnp.concatenate([counts[:, 1], first, second])
    x, *sides = attend(lat, counts, lists, cell_embed.reshape(CELLS, D), level_query,
                       query_weight, key_weight, value_weight, out_weight)
    weight = conv_weight.reshape(2, 3, 3 * D, D)
    xs, *sides = layer_step(0, lat, lat_place, (x,), *sides, weight)
    out = layer_step(1, lat, lat_place, xs, *sides, weight)
    return out.reshape(LON, LAT, LEVELS, D)


def solution(mesh):
    placed = (
        P(AXES, None), P(), P("lon", "lat", None), P(), P(AXES, None, None, None), P(AXES, None, None),
        P(), P(), P(), P(), P(),
    )
    return jax.shard_map(
        shards, mesh=mesh, in_specs=placed, out_specs=P("lon", "lat", None, None), check_vma=False
    )
```

```python
import functools
import math

import jax
import jax.numpy as jnp
from jax import lax
from jax.experimental import pallas as pl
from jax.experimental.pallas import tpu as pltpu
from jax.sharding import PartitionSpec as P

D = 512
HEADS = 16
HEAD = 32
CAP = 128
LON = 16
LAT = 32
CELLS = LON * LAT
LEVELS = 4
KEYS = 9 * CAP
SCALE = 1.0 / math.sqrt(HEAD)
LOG2E = 1.4426950408889634
CALM = 90.0
F32 = jnp.float32
BF16 = jnp.bfloat16
MIB = 1024 * 1024
NT = (((1,), (1,)), ((), ()))
TN = (((0,), (0,)), ((), ()))
AXES = ("lon", "lat")


def dot(a, b, dims=(((1,), (0,)), ((), ()))):
    return lax.dot_general(a, b, dims, preferred_element_type=F32)


def iota(shape, dim):
    return lax.broadcasted_iota(jnp.int32, shape, dim)


def gather_kernel(lat_ref, rows_hbm, embed_hbm, index_hbm, east_ref, west_ref, one_ref, two_ref, own_ref,
                  raw, held, embed_ref, index_ref, sems):
    copies = [
        pltpu.make_async_copy(rows_hbm.at[pl.ds(s * 512, 512)], raw.at[pl.ds(s * 512, 512)], sems.at[s])
        for s in range(4)
    ]
    small = [
        pltpu.make_async_copy(index_hbm, index_ref, sems.at[4]),
        pltpu.make_async_copy(embed_hbm, embed_ref, sems.at[5]),
    ]
    for copy in small + copies:
        copy.start()
    for copy in small:
        copy.wait()
    odd = lax.rem(lat_ref[0], 2)
    lanes = iota((CAP, 2048), 1)
    blocks = []
    for a in (2, 0, 1):
        picks = []
        for slot in range(3):
            if slot == 2:
                want = index_ref[3 * a + 1]
            else:
                low, high = index_ref[3 * a], index_ref[3 * a + 2]
                even_pick, odd_pick = (high, low) if slot == 0 else (low, high)
                want = jnp.where(odd == 1, odd_pick, even_pick)
            column = jnp.broadcast_to(want, (CAP, CAP)).T[:, 0:1]
            picks.append((lanes == column).astype(F32).astype(BF16))
        blocks.append(jnp.concatenate(picks, axis=0))
    for s, copy in enumerate(copies):
        copy.wait()
        span = slice(s * 512, (s + 1) * 512)
        held[span, :] = (raw[span, :].astype(F32) + embed_ref[s : s + 1, :].astype(F32)).astype(BF16)
    rows = held[...]
    east_ref[...] = dot(blocks[0], rows).astype(BF16).reshape(3, CAP, D)
    west_ref[...] = dot(blocks[1], rows).astype(BF16).reshape(3, CAP, D)
    mine = dot(blocks[2], rows).astype(BF16)
    one_ref[...] = mine[:CAP]
    two_ref[...] = mine[CAP : 2 * CAP]
    own_ref[...] = mine[2 * CAP :]


def gather(lat, patch_rows, source_embed, margin_rows):
    vmem = pl.BlockSpec(memory_space=pltpu.VMEM)
    three = jax.ShapeDtypeStruct((3, CAP, D), BF16)
    single = jax.ShapeDtypeStruct((CAP, D), BF16)
    return pl.pallas_call(
        gather_kernel,
        out_shape=(three, three, single, single, single),
        in_specs=[pl.BlockSpec(memory_space=pltpu.SMEM)] + [pl.BlockSpec(memory_space=pltpu.HBM)] * 3,
        out_specs=(vmem,) * 5,
        scratch_shapes=[
            pltpu.VMEM((2048, D), BF16), pltpu.VMEM((2048, D), BF16), pltpu.VMEM((4, D), BF16),
            pltpu.VMEM((9, 1, CAP), jnp.int32), pltpu.SemaphoreType.DMA((6,)),
        ],
        compiler_params=pltpu.CompilerParams(vmem_limit_bytes=59 * MIB),
        name="gather_rows",
    )(lat, patch_rows, source_embed, margin_rows.reshape(9, 1, CAP))


def gain_of(lat, shape, dim):
    row = (lat * LAT + iota(shape, dim)).astype(F32)
    phi = (row + 0.5) / 128 * jnp.pi - jnp.pi / 2
    return 0.5 + jnp.cos(phi)


def normal(x, gain):
    spread = jnp.sqrt(jnp.mean(x * x, axis=-1, keepdims=True) + 1e-06)
    return x / spread * gain


def edge_pick():
    row, col = iota((2 * LON, CELLS), 0), iota((2 * LON, CELLS), 1)
    return (col == row % LON * LAT + row // LON * (LAT - 1)).astype(F32).astype(BF16)


def pair_rows(lat, lev, north, south, gain, one_ref, two_ref):
    north = normal(north, gain[0:1, :])
    south = normal(south, gain[LAT - 1 :, :])
    odd = lax.rem(lat, 2) == 1
    one_ref[lev] = jnp.where(odd, north, south).astype(BF16)
    two_ref[lev] = jnp.where(odd, south, north).astype(BF16)


def head_norms(values):
    heads = (iota((D, 128), 0) // HEAD == iota((D, 128), 1)).astype(F32).astype(BF16)
    return jnp.max(dot((values * values).astype(BF16), heads), axis=0, keepdims=True)


def project_keys(rows_list, counts, wk, wv, k_s, v_s, live):
    for n, (rows, count) in enumerate(zip(rows_list, counts)):
        live[n * CAP : (n + 1) * CAP, :] = (iota((CAP, 128), 0) < count).astype(F32)
    rows = jnp.concatenate(rows_list, axis=0)
    keys = dot(rows, wk).astype(BF16)
    k_s[...] = keys
    v_s[...] = dot(rows, wv).astype(BF16)
    return head_norms(keys.astype(F32))


def head_group(hg, k_s, v_s, live, q_s, level_block):
    lanes = pl.ds(pl.multiple_of(hg * 128, 128), 128)
    kg, vg, qg = k_s[:, lanes], v_s[:, lanes], q_s[:, lanes]
    group_lane = iota((1, 128), 1) // HEAD
    col, row = iota((128, 512), 1), iota((128, 512), 0)
    copies = ((row // HEAD == col // 128) & (row % HEAD == col % HEAD)).astype(F32).astype(BF16)
    level_exp = jnp.exp2(dot(kg, level_block))
    vals = dot(vg, copies)
    alive = live[...]
    out = []
    for i in range(4):
        span = slice(i * 128, (i + 1) * 128)
        part = level_exp[:, span] * alive
        weighted = jnp.concatenate([part * vals[:, span], part], axis=1).astype(BF16)
        km = jnp.where(group_lane == i, kg, jnp.zeros_like(kg))
        probs = jnp.exp2(dot(qg, km, NT)).astype(BF16)
        out.append(dot(probs, weighted))
    return out


def list_counts(lat_ref, count_ref, part):
    odd = lax.rem(lat_ref[0], 2)
    first, second = 2 - 2 * odd, 2 * odd
    where = (
        ((1, 1), (1, first), (1, second)),
        ((0, 1), (2, 1)),
        ((0, first), (2, first), (0, second), (2, second)),
    )[part]
    return [count_ref[c, 0, r] for c, r in where]


def first_kernel(lat_ref, count_ref, own, one, two, cell_ref, level_ref, wq_ref, wk_ref, wv_ref,
                 sum_ref, q_ref, block_ref, norm_ref, k_s, v_s, live):

    counts = list_counts(lat_ref, count_ref, 0)
    norm_ref[2:3, :] = project_keys([own[...], one[...], two[...]], counts, wk_ref[...], wv_ref[...], k_s, v_s, live)
    level = jnp.concatenate([level_ref[...], level_ref[...]], axis=0)
    qc = dot(cell_ref[...], wq_ref[...]) * (SCALE * LOG2E)
    ql = dot(level, wq_ref[...]) * (SCALE * LOG2E)
    q_ref[...] = qc.astype(BF16)
    norm_ref[0:1, :] = head_norms(qc)
    norm_ref[1:2, :] = head_norms(ql)
    col, row = iota((128, 512), 1), iota((128, 512), 0)
    wide = iota((8, 512), 1)
    pick = (wide // HEAD % 4 - wide // 128 + 4) % 4
    choose = ((iota((8, 512), 0) == pick) & (iota((8, 512), 0) < 4)).astype(F32).astype(BF16)
    for g in range(4):
        spread = dot(ql[:, g * 128 : (g + 1) * 128].astype(BF16), choose, TN)
        block_ref[g] = jnp.where(row // HEAD == col // 128, spread, 0.0).astype(BF16)

    def group(hg, carry):
        for i, both in enumerate(head_group(hg, k_s, v_s, live, q_ref, block_ref[hg])):
            sum_ref[hg, i] = both
        return carry

    lax.fori_loop(0, 4, group, 0)


def second_kernel(lat_ref, count_ref, west, east, sum_in, q_ref, block_ref, wk_ref, wv_ref,
                  sum_ref, norm_ref, k_s, v_s, live):

    counts = list_counts(lat_ref, count_ref, 1)
    norm_ref[0:1, :] = project_keys([west[2], east[2]], counts, wk_ref[...], wv_ref[...], k_s, v_s, live)

    def group(hg, carry):
        for i, both in enumerate(head_group(hg, k_s, v_s, live, q_ref, block_ref[hg])):
            sum_ref[hg, i] = sum_in[hg, i] + both
        return carry

    lax.fori_loop(0, 4, group, 0)


def plain_attention(lists, counts, cell_ref, level_ref, wq_ref, wk_ref, wv_ref, k_all, v_all, q_s, live_row, att):
    for n, (rows, count) in enumerate(zip(lists, counts)):
        span = slice(n * CAP, (n + 1) * CAP)
        k_all[span, :] = dot(rows, wk_ref[...]).astype(BF16)
        v_all[span, :] = dot(rows, wv_ref[...]).astype(BF16)
        live_row[:, span] = (iota((8, CAP), 1) < count).astype(F32)
    group_lane = iota((1, 128), 1) // HEAD

    def one_level(lev, carry):
        four = level_ref[...].astype(F32)
        mine = jnp.sum(jnp.where(iota((LEVELS, D), 0) == lev, four, 0.0), axis=0, keepdims=True)
        latent = (cell_ref[...].astype(F32) + mine).astype(BF16)
        q_s[...] = dot(latent, wq_ref[...]).astype(BF16)

        def group(hg, carry):
            lanes = pl.ds(pl.multiple_of(hg * 128, 128), 128)
            kg, vg, qg = k_all[:, lanes], v_all[:, lanes], q_s[:, lanes]

            def head(i, total):
                mine = group_lane == i
                scores = dot(qg, jnp.where(mine, kg, jnp.zeros_like(kg)), NT) * SCALE
                scores = jnp.where(live_row[0:1, :] > 0.5, scores, -1e30)
                top = jnp.max(scores, axis=1, keepdims=True)
                weights = jnp.exp(scores - top)
                probs = (weights / jnp.sum(weights, axis=1, keepdims=True)).astype(BF16)
                return total + dot(probs, jnp.where(mine, vg, jnp.zeros_like(vg)))

            total = lax.fori_loop(0, 4, head, jnp.zeros((CELLS, 128), F32))
            att[lev, :, lanes] = total.astype(BF16)
            return carry

        return lax.fori_loop(0, 4, group, carry)

    lax.fori_loop(0, LEVELS, one_level, 0)


def third_kernel(lat_ref, count_ref, own, one_own, two_own, west, east, one, two, sum_in, q_ref, block_ref,
                 norm_a, norm_b, cell_ref, level_ref, wq_ref, wk_ref, wv_ref, wo_ref,
                 x_ref, west_ref, east_ref, one_ref, two_ref,
                 k_s, v_s, live, att, k_all, v_all, q_s, live_row):

    counts = list_counts(lat_ref, count_ref, 2)
    keys = project_keys([one[0], one[1], two[0], two[1]], counts, wk_ref[...], wv_ref[...], k_s, v_s, live)
    keys = jnp.maximum(jnp.maximum(keys, norm_a[2:3, :]), norm_b[0:1, :])
    bound = jnp.sqrt(norm_a[0:1, :] * keys) + jnp.sqrt(norm_a[1:2, :] * keys)
    calm = jnp.max(bound) < CALM

    @pl.when(calm)
    def _():
        group_lane = iota((1, 128), 1) // HEAD

        def group(hg, carry):
            lanes = pl.ds(pl.multiple_of(hg * 128, 128), 128)
            kept = []
            for i, both in enumerate(head_group(hg, k_s, v_s, live, q_ref, block_ref[hg])):
                both = sum_in[hg, i] + both
                kept.append(both[:, :128] / both[:, 128:])
            for lev in range(LEVELS):
                z = kept[0]
                for i in range(4):
                    z = jnp.where(group_lane == (i + lev) % 4, kept[i], z)
                if lev:
                    z = pltpu.roll(z, 128 - HEAD * lev, axis=1)
                att[lev, :, lanes] = z.astype(BF16)
            return carry

        lax.fori_loop(0, 4, group, 0)

    @pl.when(jnp.logical_not(calm))
    def _():
        lists = [own[...], one_own[...], two_own[...], west[2], east[2], one[0], one[1], two[0], two[1]]
        counts = sum((list_counts(lat_ref, count_ref, part) for part in range(3)), [])
        plain_attention(lists, counts, cell_ref, level_ref, wq_ref, wk_ref, wv_ref, k_all, v_all, q_s, live_row, att)

    gain = gain_of(lat_ref[0], (LAT, D), 0)
    pick = edge_pick()
    for lev in range(LEVELS):
        latent = (cell_ref[...].astype(F32) + level_ref[lev : lev + 1, :].astype(F32)).astype(BF16)
        x = (latent.astype(F32) + dot(att[lev], wo_ref[...])).astype(BF16)
        x_ref[lev] = x
        edge_rows = dot(pick, x)
        west_ref[lev] = normal(x[:LAT, :].astype(F32), gain).astype(BF16)
        east_ref[lev] = normal(x[CELLS - LAT :, :].astype(F32), gain).astype(BF16)
        pair_rows(lat_ref[0], lev, edge_rows[:LON], edge_rows[LON:], gain, one_ref, two_ref)


def attend_call(kernel, operands, outs, scratch, flops, alias, name):
    return call(kernel, operands, [(out, "v") for out in outs], scratch, flops, name, alias)


def part_scratch(keys):
    return [pltpu.VMEM((keys, D), BF16), pltpu.VMEM((keys, D), BF16), pltpu.VMEM((keys, 128), F32)]


def attention(lat, counts, own, one_own, two_own, exchange, cells, level_query, wq, wk, wv, wo):
    shape = jax.ShapeDtypeStruct
    sums = shape((4, 4, CELLS, 256), F32)
    norms = shape((8, 128), F32)
    each = 2 * CELLS * D * 8 * 2
    total, q, block, norm_a = attend_call(
        first_kernel,
        [(lat, "s"), (counts, "s"), (own, "v"), (one_own, "v"), (two_own, "v"), (cells, "v"), (level_query, "v"),
         (wq, "v"), (wk, "v"), (wv, "v")],
        [sums, shape((CELLS, D), BF16), shape((4, 128, 512), BF16), norms],
        part_scratch(3 * CAP), each * 3 * CAP, {}, "attend_first",
    )
    west, east, one, two = exchange(norm_a)
    total, norm_b = attend_call(
        second_kernel,
        [(lat, "s"), (counts, "s"), (west, "v"), (east, "v"), (total, "v"), (q, "v"), (block, "v"), (wk, "v"), (wv, "v")],
        [sums, norms],
        part_scratch(2 * CAP), each * 2 * CAP, {4: 0}, "attend_second",
    )
    return attend_call(
        third_kernel,
        [(lat, "s"), (counts, "s"), (own, "v"), (one_own, "v"), (two_own, "v"), (west, "v"), (east, "v"), (one, "v"),
         (two, "v"), (total, "v"), (q, "v"), (block, "v"), (norm_a, "v"), (norm_b, "v"), (cells, "v"),
         (level_query, "v"), (wq, "v"), (wk, "v"), (wv, "v"), (wo, "v")],
        [shape((LEVELS, rows, D), BF16) for rows in (CELLS, LAT, LAT, LON, LON)],
        part_scratch(4 * CAP)
        + [pltpu.VMEM((LEVELS, CELLS, D), BF16), pltpu.VMEM((KEYS, D), BF16),
           pltpu.VMEM((KEYS, D), BF16), pltpu.VMEM((CELLS, D), BF16), pltpu.VMEM((8, KEYS), F32)],
        each * 4 * CAP, {}, "attend_third",
    )


def gelu(total):
    return 0.5 * total * (1.0 + lax.erf(total * (2.0 ** -0.5)))


def read_x(x_refs, lev, low, high):
    if len(x_refs) == 1:
        return x_refs[0][lev, low * LAT : high * LAT, :].astype(F32)
    inner, inner_b, outer, rim = x_refs
    parts = []
    for lon in range(low, high):
        if 4 <= lon < 8:
            part = inner[lev, (lon - 4) * LAT : (lon - 3) * LAT, :]
        elif 8 <= lon < 12:
            part = inner_b[lev, (lon - 8) * LAT : (lon - 7) * LAT, :]
        else:
            place = lon if lon < 4 else lon - 8
            part = outer[lev, place * LAT : (place + 1) * LAT, :]
        parts.append(part.astype(F32))
    rows = jnp.concatenate(parts, axis=0).reshape(high - low, LAT, D)
    edge = rim[lev].astype(F32)
    place = iota((high - low, LAT, D), 1)
    rows = jnp.where(place == 0, edge[low:high][:, None, :], rows)
    rows = jnp.where(place == LAT - 1, edge[LON + low : LON + high][:, None, :], rows)
    return rows.reshape((high - low) * LAT, D)


def interleave(stage, start, levels):
    row, col = iota((256, 256), 0), iota((256, 256), 1)
    order = (col == row % LEVELS * 64 + row // LEVELS).astype(F32).astype(BF16)
    for half in range(2):
        rows = jnp.concatenate([y[half * 64 : half * 64 + 64] for y in levels], axis=0)
        stage[start + half * 64 : start + half * 64 + 64] = dot(order, rows).astype(BF16).reshape(64, LEVELS, D)


def three_shifts(near, wide):
    count = wide.shape[0]
    row = iota((count, D), 0) % LAT
    near[:, 0:D] = jnp.where(row == 0, 0.0, pltpu.roll(wide, 1, axis=0)).astype(BF16)
    near[:, D : 2 * D] = wide.astype(BF16)
    near[:, 2 * D :] = jnp.where(row == LAT - 1, 0.0, pltpu.roll(wide, count - 1, axis=0)).astype(BF16)


def finish(layer, total, x_refs, start, out_ref, place, stage):
    moved = gelu(total)
    levels = []
    for lev in range(LEVELS):
        levels.append((read_x(x_refs, lev, start, start + 4) + moved[lev * 128 : (lev + 1) * 128]).astype(BF16))
        if not layer:
            out_ref[lev, place : place + 128, :] = levels[lev]
    if layer:
        interleave(stage, place, levels)


def inner_kernel(layer, parts, half, lat_ref, *refs):
    x_refs, refs = refs[:parts], refs[parts:]
    w_ref, refs = refs[0], refs[1:]
    if half == 0:
        tied, out_ref, passed = refs[:3]
        refs = refs[3:]
        passed[...] = tied[...]
    elif layer:
        _, out_ref = refs[:2]
        refs = refs[2:]
    else:
        out_ref, refs = refs[0], refs[1:]
    near, stage = refs[0], refs[1:]
    start = 4 + 4 * half
    gain = gain_of(lat_ref[0], (LAT, D), 0)
    gains = jnp.concatenate([gain] * 6, axis=0)
    for lev in range(LEVELS):
        wide = normal(read_x(x_refs, lev, start - 1, start + 5), gains).astype(BF16).astype(F32)
        three_shifts(near.at[lev], wide)
    total = None
    for a in range(3):
        window = near[:, a * LAT : a * LAT + 128, :].reshape(512, 3 * D)
        part = dot(window, w_ref[layer, a])
        total = part if total is None else total + part
    finish(layer, total, x_refs, start, out_ref, 0, stage[0] if stage else None)
    if layer:
        copy = pltpu.make_async_copy(stage[0], out_ref.at[pl.ds(start * LAT, 128)], stage[1].at[0])
        copy.start()
        copy.wait()


def outer_kernel(layer, parts, lat_ref, *refs):
    x_refs, refs = refs[:parts], refs[parts:]
    west_ref, east_ref, w_ref, _ = refs[:4]
    refs = refs[4 + (1 if layer else 0) :]
    out_ref, near = refs[:2]
    stage = refs[2:]
    gain = gain_of(lat_ref[0], (LAT, D), 0)
    gains = jnp.concatenate([gain] * 5, axis=0)
    for lev in range(LEVELS):
        low = normal(read_x(x_refs, lev, 0, 5), gains).astype(BF16).astype(F32)
        three_shifts(near.at[lev, 0], jnp.concatenate([west_ref[lev].astype(F32), low], axis=0))
        high = normal(read_x(x_refs, lev, 11, 16), gains).astype(BF16).astype(F32)
        three_shifts(near.at[lev, 1], jnp.concatenate([high, east_ref[lev].astype(F32)], axis=0))
    for c in range(2):
        total = None
        for a in range(3):
            window = near[:, c, a * LAT : a * LAT + 128, :].reshape(512, 3 * D)
            part = dot(window, w_ref[layer, a])
            total = part if total is None else total + part
        finish(layer, total, x_refs, 12 * c, out_ref, 128 * c, stage[0] if stage else None)
    if layer:
        copies = [
            pltpu.make_async_copy(stage[0].at[pl.ds(0, 128)], out_ref.at[pl.ds(0, 128)], stage[1].at[0]),
            pltpu.make_async_copy(stage[0].at[pl.ds(128, 128)], out_ref.at[pl.ds(384, 128)], stage[1].at[1]),
        ]
        for copy in copies:
            copy.start()
        for copy in copies:
            copy.wait()


def rim_kernel(layer, parts, lat_ref, *refs):
    x_refs, refs = refs[:parts], refs[parts:]
    west_ref, east_ref, one_ref, two_ref, w_ref = refs[:5]
    refs = refs[5:]
    if layer:
        _, out_ref, taps, stage, stage_sems = refs
    else:
        outer_ref, rim_ref, west_out, east_out, one_out, two_out, taps = refs
    lat = lat_ref[0]
    odd = lax.rem(lat, 2) == 1
    gain = gain_of(lat, (LAT, D), 0)
    lon = iota((LON, D), 0)
    old = []
    for lev in range(LEVELS):
        row, col = iota((4 * LON, CELLS), 0), iota((4 * LON, CELLS), 1)
        lat_row = jnp.where(row < 2 * LON, row // LON, row // LON + LAT - 4)
        if parts == 1:
            pick = (col == row % LON * LAT + lat_row).astype(F32).astype(BF16)
            four = dot(pick, x_refs[0][lev])
        else:
            inner, inner_b, outer, rim = x_refs
            spot = (row % LON + 12) % LON
            spot = jnp.where(spot < 8, spot, jnp.where(spot >= 12, spot - 4, spot + 4))
            pick = (col == spot * LAT + lat_row).astype(F32).astype(BF16)
            four = dot(pick[:, :128], inner[lev]) + dot(pick[:, 128:256], inner_b[lev]) + dot(pick[:, 256:], outer[lev])
        rows = [four[n * LON : (n + 1) * LON] for n in range(4)]
        if parts > 1:
            rows[0] = rim[lev, 0:LON, :].astype(F32)
            rows[3] = rim[lev, LON:, :].astype(F32)
        old.append((rows[0], rows[3]))
        one, two = one_ref[lev].astype(F32), two_ref[lev].astype(F32)
        north = jnp.where(odd, one, two)
        south = jnp.where(odd, two, one)
        shifted = []
        for place, x in zip((0, 1, LAT - 2, LAT - 1), rows):
            u = normal(x, gain[place : place + 1, :]).astype(BF16).astype(F32)
            west = west_ref[lev, place : place + 1, :].astype(F32)
            east = east_ref[lev, place : place + 1, :].astype(F32)
            shifted.append((
                jnp.where(lon == 0, west, pltpu.roll(u, 1, axis=0)),
                u,
                jnp.where(lon == LON - 1, east, pltpu.roll(u, LON - 1, axis=0)),
            ))
        for a in range(3):
            top = jnp.concatenate([north[a : a + LON], shifted[0][a], shifted[1][a]], axis=1)
            low = jnp.concatenate([shifted[2][a], shifted[3][a], south[a : a + LON]], axis=1)
            taps[a, lev * 32 : lev * 32 + 16, :] = top.astype(BF16)
            taps[a, lev * 32 + 16 : lev * 32 + 32, :] = low.astype(BF16)
    total = None
    for a in range(3):
        part = dot(taps[a], w_ref[layer, a])
        total = part if total is None else total + part
    moved = gelu(total)
    copies = []
    for lev in range(LEVELS):
        top = (old[lev][0] + moved[lev * 32 : lev * 32 + 16]).astype(BF16)
        low = (old[lev][1] + moved[lev * 32 + 16 : lev * 32 + 32]).astype(BF16)
        if layer:
            stage[0:LON, lev, :] = top
            stage[LON:, lev, :] = low
            continue
        rim_ref[lev, 0:LON, :] = top
        rim_ref[lev, LON:, :] = low
        top, low = top.astype(F32), low.astype(F32)
        pair_rows(lat, lev, top, low, gain, one_out, two_out)
        place = iota((LAT, D), 0)
        for ref, start, k in ((west_out, 0, 0), (east_out, 7 * LAT, LON - 1)):
            column = outer_ref[lev, start : start + LAT, :].astype(F32)
            column = jnp.where(place == 0, top[k : k + 1], column)
            column = jnp.where(place == LAT - 1, low[k : k + 1], column)
            ref[lev] = normal(column, gain).astype(BF16)
    if layer:
        for k in range(LON):
            for side in range(2):
                copies.append(pltpu.make_async_copy(
                    stage.at[side * LON + k], out_ref.at[k * LAT + side * (LAT - 1)], stage_sems.at[side * LON + k]
                ))
        for copy in copies:
            copy.start()
        for copy in copies:
            copy.wait()


def corner_kernel(lat_ref, west_ref, east_ref, one_ref, two_ref, one_out, two_out):
    odd = lax.rem(lat_ref[0], 2) == 1
    for source, target, if_odd, if_even in ((one_ref, one_out, 0, LAT - 1), (two_ref, two_out, LAT - 1, 0)):
        for lev in range(LEVELS):
            ends = []
            for side in (west_ref, east_ref):
                rows = [side[lev, row : row + 1, :].astype(F32) for row in (if_odd, if_even)]
                ends.append(jnp.where(odd, rows[0], rows[1]))
            target[lev] = jnp.concatenate([ends[0], source[lev].astype(F32), ends[1]], axis=0).astype(BF16)


def pack_kernel(west_ref, east_ref, _, one_ref, two_ref):
    for slot, target in ((0, one_ref), (1, two_ref)):
        target[0] = west_ref[slot]
        target[1] = east_ref[slot]


def call(kernel, operands, outs, scratch, flops, name, alias=None):
    spaces = {"s": pltpu.SMEM, "v": pltpu.VMEM, "a": pl.ANY}
    out = pl.pallas_call(
        kernel,
        out_shape=tuple(shape for shape, _ in outs),
        in_specs=[pl.BlockSpec(memory_space=spaces[kind]) for _, kind in operands],
        out_specs=tuple(pl.BlockSpec(memory_space=spaces[kind]) for _, kind in outs),
        scratch_shapes=scratch,
        input_output_aliases=alias or {},
        compiler_params=pltpu.CompilerParams(vmem_limit_bytes=20 * MIB),
        cost_estimate=pl.CostEstimate(flops=flops, bytes_accessed=4 * MIB, transcendentals=0),
        name=name,
    )(*[array for array, _ in operands])
    return out[0] if len(out) == 1 else out


def layer_step(layer, lat, xs, west_u, east_u, one_u, two_u, weight):
    parts = len(xs)
    shape = jax.ShapeDtypeStruct
    state = [(lat, "s")] + [(x, "v") for x in xs]
    full = (shape((CELLS, LEVELS, D), BF16), "a")
    flops = 512 * 9 * D * D * 2

    def tile(rows):
        return (shape((LEVELS, rows, D), BF16), "v")

    def staging(cells, copies):
        return [pltpu.VMEM((cells, LEVELS, D), BF16), pltpu.SemaphoreType.DMA((copies,))] if layer else []

    def alias(operands):
        return {len(operands) - 1: 0} if layer else {}

    west = send(east_u, EAST)
    near = [pltpu.VMEM((LEVELS, 6 * LAT, 3 * D), BF16)]
    inner, west_u = call(
        functools.partial(inner_kernel, layer, parts, 0), state + [(weight, "v"), (west_u, "v")],
        [full if layer else tile(128), tile(LAT)], near + staging(128, 1), flops, "conv_inner",
    )
    east = send(west_u, WEST)
    operands = state + [(weight, "v")] + ([(inner, "a")] if layer else [])
    inner_b = call(
        functools.partial(inner_kernel, layer, parts, 1), operands,
        [full if layer else tile(128)], near + staging(128, 1), flops, "conv_inner", alias(operands),
    )
    one_u, two_u = call(
        corner_kernel, [(lat, "s"), (west, "v"), (east, "v"), (one_u, "v"), (two_u, "v")],
        [tile(LON + 2), tile(LON + 2)], [], 1000, "corners",
    )
    one = send(one_u, FIRST)
    two = send(two_u, SECOND)
    operands = state + [(west, "v"), (east, "v"), (weight, "v"), (one_u, "a")] + ([(inner_b, "a")] if layer else [])
    outer = call(
        functools.partial(outer_kernel, layer, parts), operands, [full if layer else tile(256)],
        [pltpu.VMEM((LEVELS, 2, 6 * LAT, 3 * D), BF16)] + staging(256, 2), 2 * flops, "conv_outer", alias(operands),
    )
    operands = state + [(west, "v"), (east, "v"), (one, "v"), (two, "v"), (weight, "v"), (outer, "a" if layer else "v")]
    done = call(
        functools.partial(rim_kernel, layer, parts), operands,
        [full] if layer else [tile(rows) for rows in (2 * LON, LAT, LAT, LON, LON)],
        [pltpu.VMEM((3, 128, 3 * D), BF16)] + staging(32, 32), flops // 4, "conv_rim", alias(operands),
    )
    return done if layer else ((inner, inner_b, outer, done[0]), *done[1:])


def route(target):
    pairs = []
    for lon in range(32):
        for lat in range(4):
            there = target(lon, lat)
            if there is not None:
                pairs.append((lon * 4 + lat, there[0] % 32 * 4 + there[1]))
    return pairs


EAST = route(lambda lon, lat: (lon + 1, lat))
WEST = route(lambda lon, lat: (lon - 1, lat))
FIRST = route(lambda lon, lat: (lon, lat ^ 1))
SECOND = route(lambda lon, lat: (lon + 16 if lat in (0, 3) else lon, (0, 2, 1, 3)[lat]))

MIDDLE = route(lambda lon, lat: (lon, 3 - lat) if lat in (1, 2) else None)


def send(block, pairs):
    return lax.ppermute(block, AXES, pairs)


def shards(
    patch_rows, source_embed, cell_embed, level_query, margin_rows, margin_counts,
    query_weight, key_weight, value_weight, out_weight, conv_weight,
):
    lat_place = lax.axis_index("lat")
    lat = lat_place.astype(jnp.int32).reshape(1)
    east_rows, west_rows, one_rows, two_rows, own = gather(lat, patch_rows, source_embed, margin_rows)
    from_west = send(east_rows, EAST)
    from_east = send(west_rows, WEST)
    one_own = send(one_rows, FIRST)
    two_own = send(two_rows, MIDDLE)

    def exchange(after):
        one, two = call(
            pack_kernel, [(from_west, "v"), (from_east, "v"), (after, "a")],
            [(jax.ShapeDtypeStruct((2, CAP, D), BF16), "v")] * 2, [], 1000, "pack",
        )
        return from_west, from_east, send(one, FIRST), send(two, MIDDLE)

    x, *sides = attention(lat, margin_counts.reshape(3, 1, 3), own, one_own, two_own, exchange,
                          cell_embed.reshape(CELLS, D), level_query, query_weight, key_weight, value_weight, out_weight)
    weight = conv_weight.reshape(2, 3, 3 * D, D)
    xs, *sides = layer_step(0, lat, (x,), *sides, weight)
    out = layer_step(1, lat, xs, *sides, weight)
    return out.reshape(LON, LAT, LEVELS, D)


def solution(mesh):
    placed = (
        P(AXES, None), P(), P("lon", "lat", None), P(), P(AXES, None, None, None), P(AXES, None, None),
        P(), P(), P(), P(), P(),
    )
    return jax.shard_map(
        shards, mesh=mesh, in_specs=placed, out_specs=P("lon", "lat", None, None), check_vma=False
    )
```

```python
import functools
import math

import jax
import jax.numpy as jnp
from jax import lax
from jax.experimental import pallas as pl
from jax.experimental.pallas import tpu as pltpu
from jax.sharding import PartitionSpec as P

D = 512
HEADS = 16
HEAD = 32
CAP = 128
LON = 16
LAT = 32
CELLS = LON * LAT
LEVELS = 4
KEYS = 9 * CAP
SCALE = 1.0 / math.sqrt(HEAD)
LOG2E = 1.4426950408889634
CALM = 90.0
F32 = jnp.float32
BF16 = jnp.bfloat16
MIB = 1024 * 1024
NT = (((1,), (1,)), ((), ()))
TN = (((0,), (0,)), ((), ()))
AXES = ("lon", "lat")


def dot(a, b, dims=(((1,), (0,)), ((), ()))):
    return lax.dot_general(a, b, dims, preferred_element_type=F32)


def iota(shape, dim):
    return lax.broadcasted_iota(jnp.int32, shape, dim)


def gather_kernel(lat_ref, rows_hbm, embed_hbm, index_hbm, east_ref, west_ref, one_ref, two_ref, own_ref,
                  raw, total, column, embed_ref, index_ref, sems):
    copies = [
        pltpu.make_async_copy(rows_hbm.at[pl.ds(s * 512, 512)], raw.at[s], sems.at[s])
        for s in range(4)
    ]
    small = [
        pltpu.make_async_copy(index_hbm, index_ref, sems.at[4]),
        pltpu.make_async_copy(embed_hbm, embed_ref, sems.at[5]),
    ]
    for copy in small + copies:
        copy.start()
    for copy in small:
        copy.wait()
    odd = lax.rem(lat_ref[0], 2)
    for n, a in enumerate((2, 0, 1)):
        for slot in range(3):
            if slot == 2:
                want = index_ref[3 * a + 1]
            else:
                low, high = index_ref[3 * a], index_ref[3 * a + 2]
                even_pick, odd_pick = (high, low) if slot == 0 else (low, high)
                want = jnp.where(odd == 1, odd_pick, even_pick)
            start = (3 * n + slot) * CAP
            column[start : start + CAP, :] = jnp.broadcast_to(want, (CAP, CAP)).T
    total[...] = jnp.zeros_like(total)
    embeds = embed_ref[...].astype(F32)

    def source(s, carry):
        pltpu.make_async_copy(rows_hbm.at[pl.ds(s * 512, 512)], raw.at[s], sems.at[s]).wait()
        embed = jnp.sum(jnp.where(iota((4, D), 0) == s, embeds, 0.0), axis=0, keepdims=True)
        rows = (raw[s].astype(F32) + embed).astype(BF16)
        local = column[...] - s * 512
        lane = iota((9 * CAP, 128), 1)
        picks = jnp.concatenate([(lane + 128 * k == local).astype(F32).astype(BF16) for k in range(4)], axis=1)
        total[...] += dot(picks, rows)
        return carry

    lax.fori_loop(0, 4, source, 0)
    three = 3 * CAP
    east_ref[...] = total[:three].astype(BF16).reshape(3, CAP, D)
    west_ref[...] = total[three : 2 * three].astype(BF16).reshape(3, CAP, D)
    one_ref[...] = total[2 * three : 2 * three + CAP].astype(BF16)
    two_ref[...] = total[2 * three + CAP : 2 * three + 2 * CAP].astype(BF16)
    own_ref[...] = total[2 * three + 2 * CAP :].astype(BF16)


def gather(lat, patch_rows, source_embed, margin_rows):
    vmem = pl.BlockSpec(memory_space=pltpu.VMEM)
    three = jax.ShapeDtypeStruct((3, CAP, D), BF16)
    single = jax.ShapeDtypeStruct((CAP, D), BF16)
    return pl.pallas_call(
        gather_kernel,
        out_shape=(three, three, single, single, single),
        in_specs=[pl.BlockSpec(memory_space=pltpu.SMEM)] + [pl.BlockSpec(memory_space=pltpu.HBM)] * 3,
        out_specs=(vmem,) * 5,
        scratch_shapes=[
            pltpu.VMEM((4, 512, D), BF16), pltpu.VMEM((9 * CAP, D), F32), pltpu.VMEM((9 * CAP, 128), jnp.int32),
            pltpu.VMEM((4, D), BF16),
            pltpu.VMEM((9, 1, CAP), jnp.int32), pltpu.SemaphoreType.DMA((6,)),
        ],
        compiler_params=pltpu.CompilerParams(vmem_limit_bytes=59 * MIB),
        name="gather_rows",
    )(lat, patch_rows, source_embed, margin_rows.reshape(9, 1, CAP))


def gain_of(lat, shape, dim):
    row = (lat * LAT + iota(shape, dim)).astype(F32)
    phi = (row + 0.5) / 128 * jnp.pi - jnp.pi / 2
    return 0.5 + jnp.cos(phi)


def normal(x, gain):
    spread = jnp.sqrt(jnp.mean(x * x, axis=-1, keepdims=True) + 1e-06)
    return x / spread * gain


def edge_pick():
    row, col = iota((2 * LON, CELLS), 0), iota((2 * LON, CELLS), 1)
    return (col == row % LON * LAT + row // LON * (LAT - 1)).astype(F32).astype(BF16)


def pair_rows(lat, lev, north, south, gain, one_ref, two_ref):
    north = normal(north, gain[0:1, :])
    south = normal(south, gain[LAT - 1 :, :])
    odd = lax.rem(lat, 2) == 1
    one_ref[lev] = jnp.where(odd, north, south).astype(BF16)
    two_ref[lev] = jnp.where(odd, south, north).astype(BF16)


def head_norms(values):
    heads = (iota((D, 128), 0) // HEAD == iota((D, 128), 1)).astype(F32).astype(BF16)
    return jnp.max(dot((values * values).astype(BF16), heads), axis=0, keepdims=True)


def project_keys(rows_list, counts, wk, wv, k_s, v_s, live):
    for n, (rows, count) in enumerate(zip(rows_list, counts)):
        live[n * CAP : (n + 1) * CAP, :] = (iota((CAP, 128), 0) < count).astype(F32)
    rows = jnp.concatenate(rows_list, axis=0)
    keys = dot(rows, wk).astype(BF16)
    k_s[...] = keys
    v_s[...] = dot(rows, wv).astype(BF16)
    return head_norms(keys.astype(F32))


def head_group(hg, k_s, v_s, live, q_s, level_block):
    lanes = pl.ds(pl.multiple_of(hg * 128, 128), 128)
    kg, vg, qg = k_s[:, lanes], v_s[:, lanes], q_s[:, lanes]
    group_lane = iota((1, 128), 1) // HEAD
    col, row = iota((128, 512), 1), iota((128, 512), 0)
    copies = ((row // HEAD == col // 128) & (row % HEAD == col % HEAD)).astype(F32).astype(BF16)
    level_exp = jnp.exp2(dot(kg, level_block))
    vals = dot(vg, copies)
    alive = live[...]
    out = []
    for i in range(4):
        span = slice(i * 128, (i + 1) * 128)
        part = level_exp[:, span] * alive
        weighted = jnp.concatenate([part * vals[:, span], part], axis=1).astype(BF16)
        km = jnp.where(group_lane == i, kg, jnp.zeros_like(kg))
        probs = jnp.exp2(dot(qg, km, NT)).astype(BF16)
        out.append(dot(probs, weighted))
    return out


def list_counts(lat_ref, count_ref, part):
    odd = lax.rem(lat_ref[0], 2)
    first, second = 2 - 2 * odd, 2 * odd
    where = (
        ((1, 1), (1, first), (1, second)),
        ((0, 1), (2, 1)),
        ((0, first), (2, first), (0, second), (2, second)),
    )[part]
    return [count_ref[c, 0, r] for c, r in where]


def first_kernel(lat_ref, count_ref, own, one, two, cell_ref, level_ref, wq_ref, wk_ref, wv_ref,
                 sum_ref, q_ref, block_ref, norm_ref, k_s, v_s, live):

    counts = list_counts(lat_ref, count_ref, 0)
    norm_ref[2:3, :] = project_keys([own[...], one[...], two[...]], counts, wk_ref[...], wv_ref[...], k_s, v_s, live)
    level = jnp.concatenate([level_ref[...], level_ref[...]], axis=0)
    qc = dot(cell_ref[...], wq_ref[...]) * (SCALE * LOG2E)
    ql = dot(level, wq_ref[...]) * (SCALE * LOG2E)
    q_ref[...] = qc.astype(BF16)
    norm_ref[0:1, :] = head_norms(qc)
    norm_ref[1:2, :] = head_norms(ql)
    col, row = iota((128, 512), 1), iota((128, 512), 0)
    wide = iota((8, 512), 1)
    pick = (wide // HEAD % 4 - wide // 128 + 4) % 4
    choose = ((iota((8, 512), 0) == pick) & (iota((8, 512), 0) < 4)).astype(F32).astype(BF16)
    for g in range(4):
        spread = dot(ql[:, g * 128 : (g + 1) * 128].astype(BF16), choose, TN)
        block_ref[g] = jnp.where(row // HEAD == col // 128, spread, 0.0).astype(BF16)

    def group(hg, carry):
        for i, both in enumerate(head_group(hg, k_s, v_s, live, q_ref, block_ref[hg])):
            sum_ref[hg, i] = both
        return carry

    lax.fori_loop(0, 4, group, 0)


def second_kernel(lat_ref, count_ref, west, east, sum_in, q_ref, block_ref, wk_ref, wv_ref,
                  sum_ref, norm_ref, k_s, v_s, live):

    counts = list_counts(lat_ref, count_ref, 1)
    norm_ref[0:1, :] = project_keys([west[2], east[2]], counts, wk_ref[...], wv_ref[...], k_s, v_s, live)

    def group(hg, carry):
        for i, both in enumerate(head_group(hg, k_s, v_s, live, q_ref, block_ref[hg])):
            sum_ref[hg, i] = sum_in[hg, i] + both
        return carry

    lax.fori_loop(0, 4, group, 0)


def plain_attention(lists, counts, cell_ref, level_ref, wq_ref, wk_ref, wv_ref, k_all, v_all, q_s, live_row, att):
    for n, (rows, count) in enumerate(zip(lists, counts)):
        span = slice(n * CAP, (n + 1) * CAP)
        k_all[span, :] = rows
        live_row[:, span] = (iota((8, CAP), 1) < count).astype(F32)

    def project(n, carry):
        span = pl.ds(pl.multiple_of(n * CAP, CAP), CAP)
        rows = k_all[span, :]
        v_all[span, :] = dot(rows, wv_ref[...]).astype(BF16)
        k_all[span, :] = dot(rows, wk_ref[...]).astype(BF16)
        return carry

    lax.fori_loop(0, 9, project, 0)
    group_lane = iota((1, 128), 1) // HEAD
    block = 128

    def step(n, carry):
        lev, part = n // 4, n % 4
        cells = pl.ds(pl.multiple_of(part * block, block), block)
        four = level_ref[...].astype(F32)
        mine = jnp.sum(jnp.where(iota((LEVELS, D), 0) == lev, four, 0.0), axis=0, keepdims=True)
        latent = (cell_ref[cells, :].astype(F32) + mine).astype(BF16)
        q_s[...] = dot(latent, wq_ref[...]).astype(BF16)

        def group(hg, carry):
            lanes = pl.ds(pl.multiple_of(hg * 128, 128), 128)
            kg, vg, qg = k_all[:, lanes], v_all[:, lanes], q_s[:, lanes]

            def head(i, total):
                mine = group_lane == i
                scores = dot(qg, jnp.where(mine, kg, jnp.zeros_like(kg)), NT) * SCALE
                scores = jnp.where(live_row[0:1, :] > 0.5, scores, -1e30)
                top = jnp.max(scores, axis=1, keepdims=True)
                weights = jnp.exp(scores - top)
                probs = (weights / jnp.sum(weights, axis=1, keepdims=True)).astype(BF16)
                return total + dot(probs, jnp.where(mine, vg, jnp.zeros_like(vg)))

            total = lax.fori_loop(0, 4, head, jnp.zeros((block, 128), F32))
            att[lev, cells, lanes] = total.astype(BF16)
            return carry

        return lax.fori_loop(0, 4, group, carry)

    lax.fori_loop(0, 4 * LEVELS, step, 0)


def third_kernel(lat_ref, count_ref, own, one_own, two_own, west, east, one, two, sum_in, q_ref, block_ref,
                 norm_a, norm_b, cell_ref, level_ref, wq_ref, wk_ref, wv_ref, wo_ref,
                 x_ref, west_ref, east_ref, one_ref, two_ref,
                 k_s, v_s, live, att, k_all, v_all, q_s, live_row):

    counts = list_counts(lat_ref, count_ref, 2)
    keys = project_keys([one[0], one[1], two[0], two[1]], counts, wk_ref[...], wv_ref[...], k_s, v_s, live)
    keys = jnp.maximum(jnp.maximum(keys, norm_a[2:3, :]), norm_b[0:1, :])
    bound = jnp.sqrt(norm_a[0:1, :] * keys) + jnp.sqrt(norm_a[1:2, :] * keys)
    calm = jnp.max(bound) < CALM

    @pl.when(calm)
    def _():
        group_lane = iota((1, 128), 1) // HEAD

        def group(hg, carry):
            lanes = pl.ds(pl.multiple_of(hg * 128, 128), 128)
            kept = []
            for i, both in enumerate(head_group(hg, k_s, v_s, live, q_ref, block_ref[hg])):
                both = sum_in[hg, i] + both
                kept.append(both[:, :128] / both[:, 128:])
            for lev in range(LEVELS):
                z = kept[0]
                for i in range(4):
                    z = jnp.where(group_lane == (i + lev) % 4, kept[i], z)
                if lev:
                    z = pltpu.roll(z, 128 - HEAD * lev, axis=1)
                att[lev, :, lanes] = z.astype(BF16)
            return carry

        lax.fori_loop(0, 4, group, 0)

    @pl.when(jnp.logical_not(calm))
    def _():
        lists = [own[...], one_own[...], two_own[...], west[2], east[2], one[0], one[1], two[0], two[1]]
        counts = sum((list_counts(lat_ref, count_ref, part) for part in range(3)), [])
        plain_attention(lists, counts, cell_ref, level_ref, wq_ref, wk_ref, wv_ref, k_all, v_all, q_s, live_row, att)

    gain = gain_of(lat_ref[0], (LAT, D), 0)
    pick = edge_pick()
    for lev in range(LEVELS):
        latent = (cell_ref[...].astype(F32) + level_ref[lev : lev + 1, :].astype(F32)).astype(BF16)
        x = (latent.astype(F32) + dot(att[lev], wo_ref[...])).astype(BF16)
        x_ref[lev] = x
        edge_rows = dot(pick, x)
        west_ref[lev] = normal(x[:LAT, :].astype(F32), gain).astype(BF16)
        east_ref[lev] = normal(x[CELLS - LAT :, :].astype(F32), gain).astype(BF16)
        pair_rows(lat_ref[0], lev, edge_rows[:LON], edge_rows[LON:], gain, one_ref, two_ref)


def attend_call(kernel, operands, outs, scratch, flops, alias, name):
    return call(kernel, operands, [(out, "v") for out in outs], scratch, flops, name, alias)


def part_scratch(keys):
    return [pltpu.VMEM((keys, D), BF16), pltpu.VMEM((keys, D), BF16), pltpu.VMEM((keys, 128), F32)]


def attention(lat, counts, own, one_own, two_own, exchange, cells, level_query, wq, wk, wv, wo):
    shape = jax.ShapeDtypeStruct
    sums = shape((4, 4, CELLS, 256), F32)
    norms = shape((8, 128), F32)
    each = 2 * CELLS * D * 8 * 2
    total, q, block, norm_a = attend_call(
        first_kernel,
        [(lat, "s"), (counts, "s"), (own, "v"), (one_own, "v"), (two_own, "v"), (cells, "v"), (level_query, "v"),
         (wq, "v"), (wk, "v"), (wv, "v")],
        [sums, shape((CELLS, D), BF16), shape((4, 128, 512), BF16), norms],
        part_scratch(3 * CAP), each * 3 * CAP, {}, "attend_first",
    )
    west, east, one, two = exchange(norm_a)
    total, norm_b = attend_call(
        second_kernel,
        [(lat, "s"), (counts, "s"), (west, "v"), (east, "v"), (total, "v"), (q, "v"), (block, "v"), (wk, "v"), (wv, "v")],
        [sums, norms],
        part_scratch(2 * CAP), each * 2 * CAP, {4: 0}, "attend_second",
    )
    return attend_call(
        third_kernel,
        [(lat, "s"), (counts, "s"), (own, "v"), (one_own, "v"), (two_own, "v"), (west, "v"), (east, "v"), (one, "v"),
         (two, "v"), (total, "v"), (q, "v"), (block, "v"), (norm_a, "v"), (norm_b, "v"), (cells, "v"),
         (level_query, "v"), (wq, "v"), (wk, "v"), (wv, "v"), (wo, "v")],
        [shape((LEVELS, rows, D), BF16) for rows in (CELLS, LAT, LAT, LON, LON)],
        part_scratch(4 * CAP)
        + [pltpu.VMEM((LEVELS, CELLS, D), BF16), pltpu.VMEM((KEYS, D), BF16),
           pltpu.VMEM((KEYS, D), BF16), pltpu.VMEM((128, D), BF16), pltpu.VMEM((8, KEYS), F32)],
        each * 4 * CAP, {}, "attend_third",
    )


def gelu(total):
    return 0.5 * total * (1.0 + lax.erf(total * (2.0 ** -0.5)))


def read_x(x_refs, lev, low, high):
    if len(x_refs) == 1:
        return x_refs[0][lev, low * LAT : high * LAT, :].astype(F32)
    inner, inner_b, outer, rim = x_refs
    parts = []
    for lon in range(low, high):
        if 4 <= lon < 8:
            part = inner[lev, (lon - 4) * LAT : (lon - 3) * LAT, :]
        elif 8 <= lon < 12:
            part = inner_b[lev, (lon - 8) * LAT : (lon - 7) * LAT, :]
        else:
            place = lon if lon < 4 else lon - 8
            part = outer[lev, place * LAT : (place + 1) * LAT, :]
        parts.append(part.astype(F32))
    rows = jnp.concatenate(parts, axis=0).reshape(high - low, LAT, D)
    edge = rim[lev].astype(F32)
    place = iota((high - low, LAT, D), 1)
    rows = jnp.where(place == 0, edge[low:high][:, None, :], rows)
    rows = jnp.where(place == LAT - 1, edge[LON + low : LON + high][:, None, :], rows)
    return rows.reshape((high - low) * LAT, D)


def interleave(stage, start, levels):
    row, col = iota((256, 256), 0), iota((256, 256), 1)
    order = (col == row % LEVELS * 64 + row // LEVELS).astype(F32).astype(BF16)
    for half in range(2):
        rows = jnp.concatenate([y[half * 64 : half * 64 + 64] for y in levels], axis=0)
        stage[start + half * 64 : start + half * 64 + 64] = dot(order, rows).astype(BF16).reshape(64, LEVELS, D)


def three_shifts(near, wide):
    count = wide.shape[0]
    row = iota((count, D), 0) % LAT
    near[:, 0:D] = jnp.where(row == 0, 0.0, pltpu.roll(wide, 1, axis=0)).astype(BF16)
    near[:, D : 2 * D] = wide.astype(BF16)
    near[:, 2 * D :] = jnp.where(row == LAT - 1, 0.0, pltpu.roll(wide, count - 1, axis=0)).astype(BF16)


def finish(layer, total, x_refs, start, out_ref, place, stage):
    moved = gelu(total)
    levels = []
    for lev in range(LEVELS):
        levels.append((read_x(x_refs, lev, start, start + 4) + moved[lev * 128 : (lev + 1) * 128]).astype(BF16))
        if not layer:
            out_ref[lev, place : place + 128, :] = levels[lev]
    if layer:
        interleave(stage, place, levels)


def inner_kernel(layer, parts, half, lat_ref, *refs):
    x_refs, refs = refs[:parts], refs[parts:]
    w_ref, refs = refs[0], refs[1:]
    if half == 0:
        tied, out_ref, passed = refs[:3]
        refs = refs[3:]
        passed[...] = tied[...]
    elif layer:
        _, out_ref = refs[:2]
        refs = refs[2:]
    else:
        out_ref, refs = refs[0], refs[1:]
    near, stage = refs[0], refs[1:]
    start = 4 + 4 * half
    gain = gain_of(lat_ref[0], (LAT, D), 0)
    gains = jnp.concatenate([gain] * 6, axis=0)
    for lev in range(LEVELS):
        wide = normal(read_x(x_refs, lev, start - 1, start + 5), gains).astype(BF16).astype(F32)
        three_shifts(near.at[lev], wide)
    total = None
    for a in range(3):
        window = near[:, a * LAT : a * LAT + 128, :].reshape(512, 3 * D)
        part = dot(window, w_ref[layer, a])
        total = part if total is None else total + part
    finish(layer, total, x_refs, start, out_ref, 0, stage[0] if stage else None)
    if layer:
        copy = pltpu.make_async_copy(stage[0], out_ref.at[pl.ds(start * LAT, 128)], stage[1].at[0])
        copy.start()
        copy.wait()


def outer_kernel(layer, parts, lat_ref, *refs):
    x_refs, refs = refs[:parts], refs[parts:]
    west_ref, east_ref, w_ref, _ = refs[:4]
    refs = refs[4 + (1 if layer else 0) :]
    out_ref, near = refs[:2]
    stage = refs[2:]
    gain = gain_of(lat_ref[0], (LAT, D), 0)
    gains = jnp.concatenate([gain] * 5, axis=0)
    for lev in range(LEVELS):
        low = normal(read_x(x_refs, lev, 0, 5), gains).astype(BF16).astype(F32)
        three_shifts(near.at[lev, 0], jnp.concatenate([west_ref[lev].astype(F32), low], axis=0))
        high = normal(read_x(x_refs, lev, 11, 16), gains).astype(BF16).astype(F32)
        three_shifts(near.at[lev, 1], jnp.concatenate([high, east_ref[lev].astype(F32)], axis=0))
    for c in range(2):
        total = None
        for a in range(3):
            window = near[:, c, a * LAT : a * LAT + 128, :].reshape(512, 3 * D)
            part = dot(window, w_ref[layer, a])
            total = part if total is None else total + part
        finish(layer, total, x_refs, 12 * c, out_ref, 128 * c, stage[0] if stage else None)
    if layer:
        copies = [
            pltpu.make_async_copy(stage[0].at[pl.ds(0, 128)], out_ref.at[pl.ds(0, 128)], stage[1].at[0]),
            pltpu.make_async_copy(stage[0].at[pl.ds(128, 128)], out_ref.at[pl.ds(384, 128)], stage[1].at[1]),
        ]
        for copy in copies:
            copy.start()
        for copy in copies:
            copy.wait()


def rim_kernel(layer, parts, lat_ref, *refs):
    x_refs, refs = refs[:parts], refs[parts:]
    west_ref, east_ref, one_ref, two_ref, w_ref = refs[:5]
    refs = refs[5:]
    if layer:
        _, out_ref, taps, stage, stage_sems = refs
    else:
        outer_ref, rim_ref, west_out, east_out, one_out, two_out, taps = refs
    lat = lat_ref[0]
    odd = lax.rem(lat, 2) == 1
    gain = gain_of(lat, (LAT, D), 0)
    lon = iota((LON, D), 0)
    old = []
    for lev in range(LEVELS):
        row, col = iota((4 * LON, CELLS), 0), iota((4 * LON, CELLS), 1)
        lat_row = jnp.where(row < 2 * LON, row // LON, row // LON + LAT - 4)
        if parts == 1:
            pick = (col == row % LON * LAT + lat_row).astype(F32).astype(BF16)
            four = dot(pick, x_refs[0][lev])
        else:
            inner, inner_b, outer, rim = x_refs
            spot = (row % LON + 12) % LON
            spot = jnp.where(spot < 8, spot, jnp.where(spot >= 12, spot - 4, spot + 4))
            pick = (col == spot * LAT + lat_row).astype(F32).astype(BF16)
            four = dot(pick[:, :128], inner[lev]) + dot(pick[:, 128:256], inner_b[lev]) + dot(pick[:, 256:], outer[lev])
        rows = [four[n * LON : (n + 1) * LON] for n in range(4)]
        if parts > 1:
            rows[0] = rim[lev, 0:LON, :].astype(F32)
            rows[3] = rim[lev, LON:, :].astype(F32)
        old.append((rows[0], rows[3]))
        one, two = one_ref[lev].astype(F32), two_ref[lev].astype(F32)
        north = jnp.where(odd, one, two)
        south = jnp.where(odd, two, one)
        shifted = []
        for place, x in zip((0, 1, LAT - 2, LAT - 1), rows):
            u = normal(x, gain[place : place + 1, :]).astype(BF16).astype(F32)
            west = west_ref[lev, place : place + 1, :].astype(F32)
            east = east_ref[lev, place : place + 1, :].astype(F32)
            shifted.append((
                jnp.where(lon == 0, west, pltpu.roll(u, 1, axis=0)),
                u,
                jnp.where(lon == LON - 1, east, pltpu.roll(u, LON - 1, axis=0)),
            ))
        for a in range(3):
            top = jnp.concatenate([north[a : a + LON], shifted[0][a], shifted[1][a]], axis=1)
            low = jnp.concatenate([shifted[2][a], shifted[3][a], south[a : a + LON]], axis=1)
            taps[a, lev * 32 : lev * 32 + 16, :] = top.astype(BF16)
            taps[a, lev * 32 + 16 : lev * 32 + 32, :] = low.astype(BF16)
    total = None
    for a in range(3):
        part = dot(taps[a], w_ref[layer, a])
        total = part if total is None else total + part
    moved = gelu(total)
    copies = []
    for lev in range(LEVELS):
        top = (old[lev][0] + moved[lev * 32 : lev * 32 + 16]).astype(BF16)
        low = (old[lev][1] + moved[lev * 32 + 16 : lev * 32 + 32]).astype(BF16)
        if layer:
            stage[0:LON, lev, :] = top
            stage[LON:, lev, :] = low
            continue
        rim_ref[lev, 0:LON, :] = top
        rim_ref[lev, LON:, :] = low
        top, low = top.astype(F32), low.astype(F32)
        pair_rows(lat, lev, top, low, gain, one_out, two_out)
        place = iota((LAT, D), 0)
        for ref, start, k in ((west_out, 0, 0), (east_out, 7 * LAT, LON - 1)):
            column = outer_ref[lev, start : start + LAT, :].astype(F32)
            column = jnp.where(place == 0, top[k : k + 1], column)
            column = jnp.where(place == LAT - 1, low[k : k + 1], column)
            ref[lev] = normal(column, gain).astype(BF16)
    if layer:
        for k in range(LON):
            for side in range(2):
                copies.append(pltpu.make_async_copy(
                    stage.at[side * LON + k], out_ref.at[k * LAT + side * (LAT - 1)], stage_sems.at[side * LON + k]
                ))
        for copy in copies:
            copy.start()
        for copy in copies:
            copy.wait()


def corner_kernel(lat_ref, west_ref, east_ref, one_ref, two_ref, one_out, two_out):
    odd = lax.rem(lat_ref[0], 2) == 1
    for source, target, if_odd, if_even in ((one_ref, one_out, 0, LAT - 1), (two_ref, two_out, LAT - 1, 0)):
        for lev in range(LEVELS):
            ends = []
            for side in (west_ref, east_ref):
                rows = [side[lev, row : row + 1, :].astype(F32) for row in (if_odd, if_even)]
                ends.append(jnp.where(odd, rows[0], rows[1]))
            target[lev] = jnp.concatenate([ends[0], source[lev].astype(F32), ends[1]], axis=0).astype(BF16)


def pack_kernel(west_ref, east_ref, _, one_ref, two_ref):
    for slot, target in ((0, one_ref), (1, two_ref)):
        target[0] = west_ref[slot]
        target[1] = east_ref[slot]


def call(kernel, operands, outs, scratch, flops, name, alias=None):
    spaces = {"s": pltpu.SMEM, "v": pltpu.VMEM, "a": pl.ANY}
    out = pl.pallas_call(
        kernel,
        out_shape=tuple(shape for shape, _ in outs),
        in_specs=[pl.BlockSpec(memory_space=spaces[kind]) for _, kind in operands],
        out_specs=tuple(pl.BlockSpec(memory_space=spaces[kind]) for _, kind in outs),
        scratch_shapes=scratch,
        input_output_aliases=alias or {},
        compiler_params=pltpu.CompilerParams(vmem_limit_bytes=20 * MIB),
        cost_estimate=pl.CostEstimate(flops=flops, bytes_accessed=4 * MIB, transcendentals=0),
        name=name,
    )(*[array for array, _ in operands])
    return out[0] if len(out) == 1 else out


def layer_step(layer, lat, xs, west_u, east_u, one_u, two_u, weight):
    parts = len(xs)
    shape = jax.ShapeDtypeStruct
    state = [(lat, "s")] + [(x, "v") for x in xs]
    full = (shape((CELLS, LEVELS, D), BF16), "a")
    flops = 512 * 9 * D * D * 2

    def tile(rows):
        return (shape((LEVELS, rows, D), BF16), "v")

    def staging(cells, copies):
        return [pltpu.VMEM((cells, LEVELS, D), BF16), pltpu.SemaphoreType.DMA((copies,))] if layer else []

    def alias(operands):
        return {len(operands) - 1: 0} if layer else {}

    west = send(east_u, EAST)
    near = [pltpu.VMEM((LEVELS, 6 * LAT, 3 * D), BF16)]
    inner, west_u = call(
        functools.partial(inner_kernel, layer, parts, 0), state + [(weight, "v"), (west_u, "v")],
        [full if layer else tile(128), tile(LAT)], near + staging(128, 1), flops, "conv_inner",
    )
    east = send(west_u, WEST)
    operands = state + [(weight, "v")] + ([(inner, "a")] if layer else [])
    inner_b = call(
        functools.partial(inner_kernel, layer, parts, 1), operands,
        [full if layer else tile(128)], near + staging(128, 1), flops, "conv_inner", alias(operands),
    )
    one_u, two_u = call(
        corner_kernel, [(lat, "s"), (west, "v"), (east, "v"), (one_u, "v"), (two_u, "v")],
        [tile(LON + 2), tile(LON + 2)], [], 1000, "corners",
    )
    one = send(one_u, FIRST)
    two = send(two_u, SECOND)
    operands = state + [(west, "v"), (east, "v"), (weight, "v"), (one_u, "a")] + ([(inner_b, "a")] if layer else [])
    outer = call(
        functools.partial(outer_kernel, layer, parts), operands, [full if layer else tile(256)],
        [pltpu.VMEM((LEVELS, 2, 6 * LAT, 3 * D), BF16)] + staging(256, 2), 2 * flops, "conv_outer", alias(operands),
    )
    operands = state + [(west, "v"), (east, "v"), (one, "v"), (two, "v"), (weight, "v"), (outer, "a" if layer else "v")]
    done = call(
        functools.partial(rim_kernel, layer, parts), operands,
        [full] if layer else [tile(rows) for rows in (2 * LON, LAT, LAT, LON, LON)],
        [pltpu.VMEM((3, 128, 3 * D), BF16)] + staging(32, 32), flops // 4, "conv_rim", alias(operands),
    )
    return done if layer else ((inner, inner_b, outer, done[0]), *done[1:])


def route(target):
    pairs = []
    for lon in range(32):
        for lat in range(4):
            there = target(lon, lat)
            if there is not None:
                pairs.append((lon * 4 + lat, there[0] % 32 * 4 + there[1]))
    return pairs


EAST = route(lambda lon, lat: (lon + 1, lat))
WEST = route(lambda lon, lat: (lon - 1, lat))
FIRST = route(lambda lon, lat: (lon, lat ^ 1))
SECOND = route(lambda lon, lat: (lon + 16 if lat in (0, 3) else lon, (0, 2, 1, 3)[lat]))

MIDDLE = route(lambda lon, lat: (lon, 3 - lat) if lat in (1, 2) else None)


def send(block, pairs):
    return lax.ppermute(block, AXES, pairs)


def shards(
    patch_rows, source_embed, cell_embed, level_query, margin_rows, margin_counts,
    query_weight, key_weight, value_weight, out_weight, conv_weight,
):
    lat_place = lax.axis_index("lat")
    lat = lat_place.astype(jnp.int32).reshape(1)
    east_rows, west_rows, one_rows, two_rows, own = gather(lat, patch_rows, source_embed, margin_rows)
    from_west = send(east_rows, EAST)
    from_east = send(west_rows, WEST)
    one_own = send(one_rows, FIRST)
    two_own = send(two_rows, MIDDLE)

    def exchange(after):
        one, two = call(
            pack_kernel, [(from_west, "v"), (from_east, "v"), (after, "a")],
            [(jax.ShapeDtypeStruct((2, CAP, D), BF16), "v")] * 2, [], 1000, "pack",
        )
        return from_west, from_east, send(one, FIRST), send(two, MIDDLE)

    x, *sides = attention(lat, margin_counts.reshape(3, 1, 3), own, one_own, two_own, exchange,
                          cell_embed.reshape(CELLS, D), level_query, query_weight, key_weight, value_weight, out_weight)
    weight = conv_weight.reshape(2, 3, 3 * D, D)
    xs, *sides = layer_step(0, lat, (x,), *sides, weight)
    out = layer_step(1, lat, xs, *sides, weight)
    return out.reshape(LON, LAT, LEVELS, D)


def solution(mesh):
    placed = (
        P(AXES, None), P(), P("lon", "lat", None), P(), P(AXES, None, None, None), P(AXES, None, None),
        P(), P(), P(), P(), P(),
    )
    return jax.shard_map(
        shards, mesh=mesh, in_specs=placed, out_specs=P("lon", "lat", None, None), check_vma=False
    )
```

```python
import functools
import math

import jax
import jax.numpy as jnp
from jax import lax
from jax.experimental import pallas as pl
from jax.experimental.pallas import tpu as pltpu
from jax.sharding import PartitionSpec as P

D = 512
HEADS = 16
HEAD = 32
CAP = 128
LON = 16
LAT = 32
CELLS = LON * LAT
LEVELS = 4
KEYS = 9 * CAP
SCALE = 1.0 / math.sqrt(HEAD)
LOG2E = 1.4426950408889634
CALM = 90.0
F32 = jnp.float32
BF16 = jnp.bfloat16
MIB = 1024 * 1024
NT = (((1,), (1,)), ((), ()))
TN = (((0,), (0,)), ((), ()))
AXES = ("lon", "lat")


def dot(a, b, dims=(((1,), (0,)), ((), ()))):
    return lax.dot_general(a, b, dims, preferred_element_type=F32)


def iota(shape, dim):
    return lax.broadcasted_iota(jnp.int32, shape, dim)


def gather_kernel(lat_ref, rows_hbm, embed_hbm, index_hbm, east_ref, west_ref, one_ref, two_ref, own_ref,
                  raw, total, column, embed_ref, index_ref, sems):
    copies = [
        pltpu.make_async_copy(rows_hbm.at[pl.ds(s * 512, 512)], raw.at[s], sems.at[s])
        for s in range(4)
    ]
    small = [
        pltpu.make_async_copy(index_hbm, index_ref, sems.at[4]),
        pltpu.make_async_copy(embed_hbm, embed_ref, sems.at[5]),
    ]
    for copy in small + copies:
        copy.start()
    for copy in small:
        copy.wait()
    odd = lax.rem(lat_ref[0], 2)
    for n, a in enumerate((2, 0, 1)):
        for slot in range(3):
            if slot == 2:
                want = index_ref[3 * a + 1]
            else:
                low, high = index_ref[3 * a], index_ref[3 * a + 2]
                even_pick, odd_pick = (high, low) if slot == 0 else (low, high)
                want = jnp.where(odd == 1, odd_pick, even_pick)
            start = (3 * n + slot) * CAP
            column[start : start + CAP, :] = jnp.broadcast_to(want, (CAP, CAP)).T
    total[...] = jnp.zeros_like(total)
    embeds = embed_ref[...].astype(F32)

    def source(s, carry):
        pltpu.make_async_copy(rows_hbm.at[pl.ds(s * 512, 512)], raw.at[s], sems.at[s]).wait()
        embed = jnp.sum(jnp.where(iota((4, D), 0) == s, embeds, 0.0), axis=0, keepdims=True)
        rows = (raw[s].astype(F32) + embed).astype(BF16)
        local = column[...] - s * 512
        lane = iota((9 * CAP, 128), 1)
        picks = jnp.concatenate([(lane + 128 * k == local).astype(F32).astype(BF16) for k in range(4)], axis=1)
        total[...] += dot(picks, rows)
        return carry

    lax.fori_loop(0, 4, source, 0)
    three = 3 * CAP
    east_ref[...] = total[:three].astype(BF16).reshape(3, CAP, D)
    west_ref[...] = total[three : 2 * three].astype(BF16).reshape(3, CAP, D)
    one_ref[...] = total[2 * three : 2 * three + CAP].astype(BF16)
    two_ref[...] = total[2 * three + CAP : 2 * three + 2 * CAP].astype(BF16)
    own_ref[...] = total[2 * three + 2 * CAP :].astype(BF16)


def gather(lat, patch_rows, source_embed, margin_rows):
    vmem = pl.BlockSpec(memory_space=pltpu.VMEM)
    three = jax.ShapeDtypeStruct((3, CAP, D), BF16)
    single = jax.ShapeDtypeStruct((CAP, D), BF16)
    return pl.pallas_call(
        gather_kernel,
        out_shape=(three, three, single, single, single),
        in_specs=[pl.BlockSpec(memory_space=pltpu.SMEM)] + [pl.BlockSpec(memory_space=pltpu.HBM)] * 3,
        out_specs=(vmem,) * 5,
        scratch_shapes=[
            pltpu.VMEM((4, 512, D), BF16), pltpu.VMEM((9 * CAP, D), F32), pltpu.VMEM((9 * CAP, 128), jnp.int32),
            pltpu.VMEM((4, D), BF16),
            pltpu.VMEM((9, 1, CAP), jnp.int32), pltpu.SemaphoreType.DMA((6,)),
        ],
        compiler_params=pltpu.CompilerParams(vmem_limit_bytes=59 * MIB),
        name="gather_rows",
    )(lat, patch_rows, source_embed, margin_rows.reshape(9, 1, CAP))


def gain_of(lat, shape, dim):
    row = (lat * LAT + iota(shape, dim)).astype(F32)
    phi = (row + 0.5) / 128 * jnp.pi - jnp.pi / 2
    return 0.5 + jnp.cos(phi)


def normal(x, gain):
    spread = jnp.sqrt(jnp.mean(x * x, axis=-1, keepdims=True) + 1e-06)
    return x / spread * gain


def edge_pick():
    row, col = iota((2 * LON, CELLS), 0), iota((2 * LON, CELLS), 1)
    return (col == row % LON * LAT + row // LON * (LAT - 1)).astype(F32).astype(BF16)


def pair_rows(lat, lev, north, south, gain, one_ref, two_ref):
    north = normal(north, gain[0:1, :])
    south = normal(south, gain[LAT - 1 :, :])
    odd = lax.rem(lat, 2) == 1
    one_ref[lev] = jnp.where(odd, north, south).astype(BF16)
    two_ref[lev] = jnp.where(odd, south, north).astype(BF16)


def head_norms(values):
    heads = (iota((D, 128), 0) // HEAD == iota((D, 128), 1)).astype(F32).astype(BF16)
    return jnp.max(dot((values * values).astype(BF16), heads), axis=0, keepdims=True)


def project_keys(rows_list, counts, wk, wv, k_s, v_s, live):
    for n, (rows, count) in enumerate(zip(rows_list, counts)):
        live[n * CAP : (n + 1) * CAP, :] = (iota((CAP, 128), 0) < count).astype(F32)
    rows = jnp.concatenate(rows_list, axis=0)
    keys = dot(rows, wk).astype(BF16)
    k_s[...] = keys
    v_s[...] = dot(rows, wv).astype(BF16)
    return head_norms(keys.astype(F32))


def head_group(hg, k_s, v_s, live, q_s, level_block):
    lanes = pl.ds(pl.multiple_of(hg * 128, 128), 128)
    kg, vg, qg = k_s[:, lanes], v_s[:, lanes], q_s[:, lanes]
    group_lane = iota((1, 128), 1) // HEAD
    col, row = iota((128, 512), 1), iota((128, 512), 0)
    copies = ((row // HEAD == col // 128) & (row % HEAD == col % HEAD)).astype(F32).astype(BF16)
    level_exp = jnp.exp2(dot(kg, level_block))
    vals = dot(vg, copies)
    alive = live[...]
    out = []
    for i in range(4):
        span = slice(i * 128, (i + 1) * 128)
        part = level_exp[:, span] * alive
        weighted = jnp.concatenate([part * vals[:, span], part], axis=1).astype(BF16)
        km = jnp.where(group_lane == i, kg, jnp.zeros_like(kg))
        probs = jnp.exp2(dot(qg, km, NT)).astype(BF16)
        out.append(dot(probs, weighted))
    return out


def list_counts(lat_ref, count_ref, part):
    odd = lax.rem(lat_ref[0], 2)
    first, second = 2 - 2 * odd, 2 * odd
    where = (
        ((1, 1), (1, first), (1, second)),
        ((0, 1), (2, 1)),
        ((0, first), (2, first), (0, second), (2, second)),
    )[part]
    return [count_ref[c, 0, r] for c, r in where]


def first_kernel(lat_ref, count_ref, own, one, two, cell_ref, level_ref, wq_ref, wk_ref, wv_ref,
                 sum_ref, q_ref, block_ref, norm_ref, k_s, v_s, live):

    counts = list_counts(lat_ref, count_ref, 0)
    norm_ref[2:3, :] = project_keys([own[...], one[...], two[...]], counts, wk_ref[...], wv_ref[...], k_s, v_s, live)
    level = jnp.concatenate([level_ref[...], level_ref[...]], axis=0)
    qc = dot(cell_ref[...], wq_ref[...]) * (SCALE * LOG2E)
    ql = dot(level, wq_ref[...]) * (SCALE * LOG2E)
    q_ref[...] = qc.astype(BF16)
    norm_ref[0:1, :] = head_norms(qc)
    norm_ref[1:2, :] = head_norms(ql)
    col, row = iota((128, 512), 1), iota((128, 512), 0)
    wide = iota((8, 512), 1)
    pick = (wide // HEAD % 4 - wide // 128 + 4) % 4
    choose = ((iota((8, 512), 0) == pick) & (iota((8, 512), 0) < 4)).astype(F32).astype(BF16)
    for g in range(4):
        spread = dot(ql[:, g * 128 : (g + 1) * 128].astype(BF16), choose, TN)
        block_ref[g] = jnp.where(row // HEAD == col // 128, spread, 0.0).astype(BF16)

    def group(hg, carry):
        for i, both in enumerate(head_group(hg, k_s, v_s, live, q_ref, block_ref[hg])):
            sum_ref[hg, i] = both
        return carry

    lax.fori_loop(0, 4, group, 0)


def second_kernel(lat_ref, count_ref, west, east, sum_in, q_ref, block_ref, wk_ref, wv_ref,
                  sum_ref, norm_ref, k_s, v_s, live):

    counts = list_counts(lat_ref, count_ref, 1)
    norm_ref[0:1, :] = project_keys([west[2], east[2]], counts, wk_ref[...], wv_ref[...], k_s, v_s, live)

    def group(hg, carry):
        for i, both in enumerate(head_group(hg, k_s, v_s, live, q_ref, block_ref[hg])):
            sum_ref[hg, i] = sum_in[hg, i] + both
        return carry

    lax.fori_loop(0, 4, group, 0)


def plain_attention(lists, counts, cell_ref, level_ref, wq_ref, wk_ref, wv_ref, k_all, v_all, q_s, live_row, att):
    for n, (rows, count) in enumerate(zip(lists, counts)):
        span = slice(n * CAP, (n + 1) * CAP)
        k_all[span, :] = rows
        live_row[:, span] = (iota((8, CAP), 1) < count).astype(F32)

    def project(n, carry):
        span = pl.ds(pl.multiple_of(n * CAP, CAP), CAP)
        rows = k_all[span, :]
        v_all[span, :] = dot(rows, wv_ref[...]).astype(BF16)
        k_all[span, :] = dot(rows, wk_ref[...]).astype(BF16)
        return carry

    lax.fori_loop(0, 9, project, 0)
    group_lane = iota((1, 128), 1) // HEAD
    block = 128

    def step(n, carry):
        lev, part = n // 4, n % 4
        cells = pl.ds(pl.multiple_of(part * block, block), block)
        four = level_ref[...].astype(F32)
        mine = jnp.sum(jnp.where(iota((LEVELS, D), 0) == lev, four, 0.0), axis=0, keepdims=True)
        latent = (cell_ref[cells, :].astype(F32) + mine).astype(BF16)
        q_s[...] = dot(latent, wq_ref[...]).astype(BF16)

        def group(hg, carry):
            lanes = pl.ds(pl.multiple_of(hg * 128, 128), 128)
            kg, vg, qg = k_all[:, lanes], v_all[:, lanes], q_s[:, lanes]

            def head(i, total):
                mine = group_lane == i
                scores = dot(qg, jnp.where(mine, kg, jnp.zeros_like(kg)), NT) * SCALE
                scores = jnp.where(live_row[0:1, :] > 0.5, scores, -1e30)
                top = jnp.max(scores, axis=1, keepdims=True)
                weights = jnp.exp(scores - top)
                probs = (weights / jnp.sum(weights, axis=1, keepdims=True)).astype(BF16)
                return total + dot(probs, jnp.where(mine, vg, jnp.zeros_like(vg)))

            total = lax.fori_loop(0, 4, head, jnp.zeros((block, 128), F32))
            att[lev, cells, lanes] = total.astype(BF16)
            return carry

        return lax.fori_loop(0, 4, group, carry)

    lax.fori_loop(0, 4 * LEVELS, step, 0)


def third_kernel(lat_ref, count_ref, own, one_own, two_own, west, east, one, two, sum_in, q_ref, block_ref,
                 norm_a, norm_b, cell_ref, level_ref, wq_ref, wk_ref, wv_ref, wo_ref,
                 x_ref, west_ref, east_ref, one_ref, two_ref,
                 k_s, v_s, live, att, k_all, v_all, q_s, live_row):

    counts = list_counts(lat_ref, count_ref, 2)
    keys = project_keys([one[0], one[1], two[0], two[1]], counts, wk_ref[...], wv_ref[...], k_s, v_s, live)
    keys = jnp.maximum(jnp.maximum(keys, norm_a[2:3, :]), norm_b[0:1, :])
    bound = jnp.sqrt(norm_a[0:1, :] * keys) + jnp.sqrt(norm_a[1:2, :] * keys)
    calm = jnp.max(bound) < CALM

    @pl.when(calm)
    def _():
        group_lane = iota((1, 128), 1) // HEAD

        def group(hg, carry):
            lanes = pl.ds(pl.multiple_of(hg * 128, 128), 128)
            kept = []
            for i, both in enumerate(head_group(hg, k_s, v_s, live, q_ref, block_ref[hg])):
                both = sum_in[hg, i] + both
                kept.append(both[:, :128] / both[:, 128:])
            for lev in range(LEVELS):
                z = kept[0]
                for i in range(4):
                    z = jnp.where(group_lane == (i + lev) % 4, kept[i], z)
                if lev:
                    z = pltpu.roll(z, 128 - HEAD * lev, axis=1)
                att[lev, :, lanes] = z.astype(BF16)
            return carry

        lax.fori_loop(0, 4, group, 0)

    @pl.when(jnp.logical_not(calm))
    def _():
        lists = [own[...], one_own[...], two_own[...], west[2], east[2], one[0], one[1], two[0], two[1]]
        counts = sum((list_counts(lat_ref, count_ref, part) for part in range(3)), [])
        plain_attention(lists, counts, cell_ref, level_ref, wq_ref, wk_ref, wv_ref, k_all, v_all, q_s, live_row, att)

    gain = gain_of(lat_ref[0], (LAT, D), 0)
    pick = edge_pick()
    for lev in range(LEVELS):
        latent = (cell_ref[...].astype(F32) + level_ref[lev : lev + 1, :].astype(F32)).astype(BF16)
        x = (latent.astype(F32) + dot(att[lev], wo_ref[...])).astype(BF16)
        x_ref[lev] = x
        edge_rows = dot(pick, x)
        west_ref[lev] = normal(x[:LAT, :].astype(F32), gain).astype(BF16)
        east_ref[lev] = normal(x[CELLS - LAT :, :].astype(F32), gain).astype(BF16)
        pair_rows(lat_ref[0], lev, edge_rows[:LON], edge_rows[LON:], gain, one_ref, two_ref)


def attend_call(kernel, operands, outs, scratch, flops, alias, name):
    return call(kernel, operands, [(out, "v") for out in outs], scratch, flops, name, alias)


def part_scratch(keys):
    return [pltpu.VMEM((keys, D), BF16), pltpu.VMEM((keys, D), BF16), pltpu.VMEM((keys, 128), F32)]


def attention(lat, counts, own, one_own, two_own, exchange, cells, level_query, wq, wk, wv, wo):
    shape = jax.ShapeDtypeStruct
    sums = shape((4, 4, CELLS, 256), F32)
    norms = shape((8, 128), F32)
    each = 2 * CELLS * D * 8 * 2
    total, q, block, norm_a = attend_call(
        first_kernel,
        [(lat, "s"), (counts, "s"), (own, "v"), (one_own, "v"), (two_own, "v"), (cells, "v"), (level_query, "v"),
         (wq, "v"), (wk, "v"), (wv, "v")],
        [sums, shape((CELLS, D), BF16), shape((4, 128, 512), BF16), norms],
        part_scratch(3 * CAP), each * 3 * CAP, {}, "attend_first",
    )
    west, east, one, two = exchange(norm_a)
    total, norm_b = attend_call(
        second_kernel,
        [(lat, "s"), (counts, "s"), (west, "v"), (east, "v"), (total, "v"), (q, "v"), (block, "v"), (wk, "v"), (wv, "v")],
        [sums, norms],
        part_scratch(2 * CAP), each * 2 * CAP, {4: 0}, "attend_second",
    )
    return attend_call(
        third_kernel,
        [(lat, "s"), (counts, "s"), (own, "v"), (one_own, "v"), (two_own, "v"), (west, "v"), (east, "v"), (one, "v"),
         (two, "v"), (total, "v"), (q, "v"), (block, "v"), (norm_a, "v"), (norm_b, "v"), (cells, "v"),
         (level_query, "v"), (wq, "v"), (wk, "v"), (wv, "v"), (wo, "v")],
        [shape((LEVELS, rows, D), BF16) for rows in (CELLS, LAT, LAT, LON, LON)],
        part_scratch(4 * CAP)
        + [pltpu.VMEM((LEVELS, CELLS, D), BF16), pltpu.VMEM((KEYS, D), BF16),
           pltpu.VMEM((KEYS, D), BF16), pltpu.VMEM((128, D), BF16), pltpu.VMEM((8, KEYS), F32)],
        each * 4 * CAP, {}, "attend_third",
    )


def gelu(total):
    return 0.5 * total * (1.0 + lax.erf(total * (2.0 ** -0.5)))


def read_x(x_refs, lev, low, high):
    if len(x_refs) == 1:
        return x_refs[0][lev, low * LAT : high * LAT, :].astype(F32)
    inner, inner_b, outer, rim = x_refs
    parts = []
    for lon in range(low, high):
        if 4 <= lon < 8:
            part = inner[lev, (lon - 4) * LAT : (lon - 3) * LAT, :]
        elif 8 <= lon < 12:
            part = inner_b[lev, (lon - 8) * LAT : (lon - 7) * LAT, :]
        else:
            place = lon if lon < 4 else lon - 8
            part = outer[lev, place * LAT : (place + 1) * LAT, :]
        parts.append(part.astype(F32))
    rows = jnp.concatenate(parts, axis=0).reshape(high - low, LAT, D)
    edge = rim[lev].astype(F32)
    place = iota((high - low, LAT, D), 1)
    rows = jnp.where(place == 0, edge[low:high][:, None, :], rows)
    rows = jnp.where(place == LAT - 1, edge[LON + low : LON + high][:, None, :], rows)
    return rows.reshape((high - low) * LAT, D)


def interleave(stage, start, levels, after):
    row, col = iota((256, 256), 0), iota((256, 256), 1)
    order = (col == row % LEVELS * 64 + row // LEVELS).astype(F32).astype(BF16)
    for half in range(2):
        rows = jnp.concatenate([y[half * 64 : half * 64 + 64] for y in levels], axis=0)
        stage[start + half * 64 : start + half * 64 + 64] = dot(order, rows).astype(BF16).reshape(64, LEVELS, D)
        after(start + half * 64)


def three_shifts(near, wide):
    count = wide.shape[0]
    row = iota((count, D), 0) % LAT
    near[:, 0:D] = jnp.where(row == 0, 0.0, pltpu.roll(wide, 1, axis=0)).astype(BF16)
    near[:, D : 2 * D] = wide.astype(BF16)
    near[:, 2 * D :] = jnp.where(row == LAT - 1, 0.0, pltpu.roll(wide, count - 1, axis=0)).astype(BF16)


def finish(layer, total, x_refs, start, out_ref, place, stage, after):
    moved = gelu(total)
    levels = []
    for lev in range(LEVELS):
        levels.append((read_x(x_refs, lev, start, start + 4) + moved[lev * 128 : (lev + 1) * 128]).astype(BF16))
        if not layer:
            out_ref[lev, place : place + 128, :] = levels[lev]
    if layer:
        interleave(stage, place, levels, after)


def inner_kernel(layer, parts, half, lat_ref, *refs):
    x_refs, refs = refs[:parts], refs[parts:]
    w_ref, refs = refs[0], refs[1:]
    if half == 0:
        tied, out_ref, passed = refs[:3]
        refs = refs[3:]
        passed[...] = tied[...]
    elif layer:
        _, out_ref = refs[:2]
        refs = refs[2:]
    else:
        out_ref, refs = refs[0], refs[1:]
    near, stage = refs[0], refs[1:]
    start = 4 + 4 * half
    gain = gain_of(lat_ref[0], (LAT, D), 0)
    gains = jnp.concatenate([gain] * 6, axis=0)
    for lev in range(LEVELS):
        wide = normal(read_x(x_refs, lev, start - 1, start + 5), gains).astype(BF16).astype(F32)
        three_shifts(near.at[lev], wide)
    total = None
    for a in range(3):
        window = near[:, a * LAT : a * LAT + 128, :].reshape(512, 3 * D)
        part = dot(window, w_ref[layer, a])
        total = part if total is None else total + part
    copies = []

    def after(place):
        copies.append(pltpu.make_async_copy(
            stage[0].at[pl.ds(place, 64)], out_ref.at[pl.ds(start * LAT + place, 64)], stage[1].at[len(copies)]
        ))
        copies[-1].start()

    finish(layer, total, x_refs, start, out_ref, 0, stage[0] if stage else None, after)
    for copy in copies:
        copy.wait()


def outer_kernel(layer, parts, lat_ref, *refs):
    x_refs, refs = refs[:parts], refs[parts:]
    west_ref, east_ref, w_ref, _ = refs[:4]
    refs = refs[4 + (1 if layer else 0) :]
    out_ref, near = refs[:2]
    stage = refs[2:]
    gain = gain_of(lat_ref[0], (LAT, D), 0)
    gains = jnp.concatenate([gain] * 5, axis=0)
    for lev in range(LEVELS):
        low = normal(read_x(x_refs, lev, 0, 5), gains).astype(BF16).astype(F32)
        three_shifts(near.at[lev, 0], jnp.concatenate([west_ref[lev].astype(F32), low], axis=0))
        high = normal(read_x(x_refs, lev, 11, 16), gains).astype(BF16).astype(F32)
        three_shifts(near.at[lev, 1], jnp.concatenate([high, east_ref[lev].astype(F32)], axis=0))
    copies = []

    def after(place):
        target = place if place < 128 else place + 256
        copies.append(pltpu.make_async_copy(
            stage[0].at[pl.ds(place, 64)], out_ref.at[pl.ds(target, 64)], stage[1].at[len(copies)]
        ))
        copies[-1].start()

    for c in range(2):
        total = None
        for a in range(3):
            window = near[:, c, a * LAT : a * LAT + 128, :].reshape(512, 3 * D)
            part = dot(window, w_ref[layer, a])
            total = part if total is None else total + part
        finish(layer, total, x_refs, 12 * c, out_ref, 128 * c, stage[0] if stage else None, after)
    for copy in copies:
        copy.wait()


def rim_kernel(layer, parts, lat_ref, *refs):
    x_refs, refs = refs[:parts], refs[parts:]
    west_ref, east_ref, one_ref, two_ref, w_ref = refs[:5]
    refs = refs[5:]
    if layer:
        _, out_ref, taps, stage, stage_sems = refs
    else:
        outer_ref, rim_ref, west_out, east_out, one_out, two_out, taps = refs
    lat = lat_ref[0]
    odd = lax.rem(lat, 2) == 1
    gain = gain_of(lat, (LAT, D), 0)
    lon = iota((LON, D), 0)
    old = []
    for lev in range(LEVELS):
        row, col = iota((4 * LON, CELLS), 0), iota((4 * LON, CELLS), 1)
        lat_row = jnp.where(row < 2 * LON, row // LON, row // LON + LAT - 4)
        if parts == 1:
            pick = (col == row % LON * LAT + lat_row).astype(F32).astype(BF16)
            four = dot(pick, x_refs[0][lev])
        else:
            inner, inner_b, outer, rim = x_refs
            spot = (row % LON + 12) % LON
            spot = jnp.where(spot < 8, spot, jnp.where(spot >= 12, spot - 4, spot + 4))
            pick = (col == spot * LAT + lat_row).astype(F32).astype(BF16)
            four = dot(pick[:, :128], inner[lev]) + dot(pick[:, 128:256], inner_b[lev]) + dot(pick[:, 256:], outer[lev])
        rows = [four[n * LON : (n + 1) * LON] for n in range(4)]
        if parts > 1:
            rows[0] = rim[lev, 0:LON, :].astype(F32)
            rows[3] = rim[lev, LON:, :].astype(F32)
        old.append((rows[0], rows[3]))
        one, two = one_ref[lev].astype(F32), two_ref[lev].astype(F32)
        north = jnp.where(odd, one, two)
        south = jnp.where(odd, two, one)
        shifted = []
        for place, x in zip((0, 1, LAT - 2, LAT - 1), rows):
            u = normal(x, gain[place : place + 1, :]).astype(BF16).astype(F32)
            west = west_ref[lev, place : place + 1, :].astype(F32)
            east = east_ref[lev, place : place + 1, :].astype(F32)
            shifted.append((
                jnp.where(lon == 0, west, pltpu.roll(u, 1, axis=0)),
                u,
                jnp.where(lon == LON - 1, east, pltpu.roll(u, LON - 1, axis=0)),
            ))
        for a in range(3):
            top = jnp.concatenate([north[a : a + LON], shifted[0][a], shifted[1][a]], axis=1)
            low = jnp.concatenate([shifted[2][a], shifted[3][a], south[a : a + LON]], axis=1)
            taps[a, lev * 32 : lev * 32 + 16, :] = top.astype(BF16)
            taps[a, lev * 32 + 16 : lev * 32 + 32, :] = low.astype(BF16)
    total = None
    for a in range(3):
        part = dot(taps[a], w_ref[layer, a])
        total = part if total is None else total + part
    moved = gelu(total)
    copies = []
    for lev in range(LEVELS):
        top = (old[lev][0] + moved[lev * 32 : lev * 32 + 16]).astype(BF16)
        low = (old[lev][1] + moved[lev * 32 + 16 : lev * 32 + 32]).astype(BF16)
        if layer:
            stage[0:LON, lev, :] = top
            stage[LON:, lev, :] = low
            continue
        rim_ref[lev, 0:LON, :] = top
        rim_ref[lev, LON:, :] = low
        top, low = top.astype(F32), low.astype(F32)
        pair_rows(lat, lev, top, low, gain, one_out, two_out)
        place = iota((LAT, D), 0)
        for ref, start, k in ((west_out, 0, 0), (east_out, 7 * LAT, LON - 1)):
            column = outer_ref[lev, start : start + LAT, :].astype(F32)
            column = jnp.where(place == 0, top[k : k + 1], column)
            column = jnp.where(place == LAT - 1, low[k : k + 1], column)
            ref[lev] = normal(column, gain).astype(BF16)
    if layer:
        for k in range(LON):
            for side in range(2):
                copies.append(pltpu.make_async_copy(
                    stage.at[side * LON + k], out_ref.at[k * LAT + side * (LAT - 1)], stage_sems.at[side * LON + k]
                ))
        for copy in copies:
            copy.start()
        for copy in copies:
            copy.wait()


def corner_kernel(lat_ref, west_ref, east_ref, one_ref, two_ref, one_out, two_out):
    odd = lax.rem(lat_ref[0], 2) == 1
    for source, target, if_odd, if_even in ((one_ref, one_out, 0, LAT - 1), (two_ref, two_out, LAT - 1, 0)):
        for lev in range(LEVELS):
            ends = []
            for side in (west_ref, east_ref):
                rows = [side[lev, row : row + 1, :].astype(F32) for row in (if_odd, if_even)]
                ends.append(jnp.where(odd, rows[0], rows[1]))
            target[lev] = jnp.concatenate([ends[0], source[lev].astype(F32), ends[1]], axis=0).astype(BF16)


def pack_kernel(west_ref, east_ref, _, one_ref, two_ref):
    for slot, target in ((0, one_ref), (1, two_ref)):
        target[0] = west_ref[slot]
        target[1] = east_ref[slot]


def call(kernel, operands, outs, scratch, flops, name, alias=None):
    spaces = {"s": pltpu.SMEM, "v": pltpu.VMEM, "a": pl.ANY}
    out = pl.pallas_call(
        kernel,
        out_shape=tuple(shape for shape, _ in outs),
        in_specs=[pl.BlockSpec(memory_space=spaces[kind]) for _, kind in operands],
        out_specs=tuple(pl.BlockSpec(memory_space=spaces[kind]) for _, kind in outs),
        scratch_shapes=scratch,
        input_output_aliases=alias or {},
        compiler_params=pltpu.CompilerParams(vmem_limit_bytes=20 * MIB),
        cost_estimate=pl.CostEstimate(flops=flops, bytes_accessed=4 * MIB, transcendentals=0),
        name=name,
    )(*[array for array, _ in operands])
    return out[0] if len(out) == 1 else out


def layer_step(layer, lat, xs, west_u, east_u, one_u, two_u, weight):
    parts = len(xs)
    shape = jax.ShapeDtypeStruct
    state = [(lat, "s")] + [(x, "v") for x in xs]
    full = (shape((CELLS, LEVELS, D), BF16), "a")
    flops = 512 * 9 * D * D * 2

    def tile(rows):
        return (shape((LEVELS, rows, D), BF16), "v")

    def staging(cells, copies):
        return [pltpu.VMEM((cells, LEVELS, D), BF16), pltpu.SemaphoreType.DMA((copies,))] if layer else []

    def alias(operands):
        return {len(operands) - 1: 0} if layer else {}

    west = send(east_u, EAST)
    near = [pltpu.VMEM((LEVELS, 6 * LAT, 3 * D), BF16)]
    inner, west_u = call(
        functools.partial(inner_kernel, layer, parts, 0), state + [(weight, "v"), (west_u, "v")],
        [full if layer else tile(128), tile(LAT)], near + staging(128, 2), flops, "conv_inner",
    )
    east = send(west_u, WEST)
    operands = state + [(weight, "v")] + ([(inner, "a")] if layer else [])
    inner_b = call(
        functools.partial(inner_kernel, layer, parts, 1), operands,
        [full if layer else tile(128)], near + staging(128, 2), flops, "conv_inner", alias(operands),
    )
    one_u, two_u = call(
        corner_kernel, [(lat, "s"), (west, "v"), (east, "v"), (one_u, "v"), (two_u, "v")],
        [tile(LON + 2), tile(LON + 2)], [], 1000, "corners",
    )
    one = send(one_u, FIRST)
    two = send(two_u, SECOND)
    operands = state + [(west, "v"), (east, "v"), (weight, "v"), (one_u, "a")] + ([(inner_b, "a")] if layer else [])
    outer = call(
        functools.partial(outer_kernel, layer, parts), operands, [full if layer else tile(256)],
        [pltpu.VMEM((LEVELS, 2, 6 * LAT, 3 * D), BF16)] + staging(256, 4), 2 * flops, "conv_outer", alias(operands),
    )
    operands = state + [(west, "v"), (east, "v"), (one, "v"), (two, "v"), (weight, "v"), (outer, "a" if layer else "v")]
    done = call(
        functools.partial(rim_kernel, layer, parts), operands,
        [full] if layer else [tile(rows) for rows in (2 * LON, LAT, LAT, LON, LON)],
        [pltpu.VMEM((3, 128, 3 * D), BF16)] + staging(32, 32), flops // 4, "conv_rim", alias(operands),
    )
    return done if layer else ((inner, inner_b, outer, done[0]), *done[1:])


def route(target):
    pairs = []
    for lon in range(32):
        for lat in range(4):
            there = target(lon, lat)
            if there is not None:
                pairs.append((lon * 4 + lat, there[0] % 32 * 4 + there[1]))
    return pairs


EAST = route(lambda lon, lat: (lon + 1, lat))
WEST = route(lambda lon, lat: (lon - 1, lat))
FIRST = route(lambda lon, lat: (lon, lat ^ 1))
SECOND = route(lambda lon, lat: (lon + 16 if lat in (0, 3) else lon, (0, 2, 1, 3)[lat]))

MIDDLE = route(lambda lon, lat: (lon, 3 - lat) if lat in (1, 2) else None)


def send(block, pairs):
    return lax.ppermute(block, AXES, pairs)


def shards(
    patch_rows, source_embed, cell_embed, level_query, margin_rows, margin_counts,
    query_weight, key_weight, value_weight, out_weight, conv_weight,
):
    lat_place = lax.axis_index("lat")
    lat = lat_place.astype(jnp.int32).reshape(1)
    east_rows, west_rows, one_rows, two_rows, own = gather(lat, patch_rows, source_embed, margin_rows)
    from_west = send(east_rows, EAST)
    from_east = send(west_rows, WEST)
    one_own = send(one_rows, FIRST)
    two_own = send(two_rows, MIDDLE)

    def exchange(after):
        one, two = call(
            pack_kernel, [(from_west, "v"), (from_east, "v"), (after, "a")],
            [(jax.ShapeDtypeStruct((2, CAP, D), BF16), "v")] * 2, [], 1000, "pack",
        )
        return from_west, from_east, send(one, FIRST), send(two, MIDDLE)

    x, *sides = attention(lat, margin_counts.reshape(3, 1, 3), own, one_own, two_own, exchange,
                          cell_embed.reshape(CELLS, D), level_query, query_weight, key_weight, value_weight, out_weight)
    weight = conv_weight.reshape(2, 3, 3 * D, D)
    xs, *sides = layer_step(0, lat, (x,), *sides, weight)
    out = layer_step(1, lat, xs, *sides, weight)
    return out.reshape(LON, LAT, LEVELS, D)


def solution(mesh):
    placed = (
        P(AXES, None), P(), P("lon", "lat", None), P(), P(AXES, None, None, None), P(AXES, None, None),
        P(), P(), P(), P(), P(),
    )
    return jax.shard_map(
        shards, mesh=mesh, in_specs=placed, out_specs=P("lon", "lat", None, None), check_vma=False
    )
```
